256 devices in a mesh: wrap: 16 (over x, y_hi, core), inst: 16 (over y_lo, z).
Axes of the slice: x: 4, y: 4 (y_hi: 2, y_lo: 2; y = y_hi * 2 + y_lo), z: 8, core: 2. Of those that a mesh axis runs over, the one named last changes fastest.
Arguments:
- state: float32 [32, 6, 8, 512, 128], P('inst', None, None, 'wrap'), may hold values from -0.8 to 3.3, as said below
- metrics: float32 [3, 3, 8, 512, 128], P(None, None, None, 'wrap'), may hold values from -3 to 3
- volume: float32 [8, 512, 128], P(None, 'wrap'), may hold values from 0.5 to 2
Outputs:
- residual: float32 [32, 6, 8, 512, 128], P('inst', None, None, 'wrap')
The draws below stay inside these ranges and needn't reach their ends.
Inputs may be any that keep to these rules, and one draw needn't show every extreme that they name: Every instance and cell holds a physical state: density from 0.7 to 1.3, speed below 1.1, pressure from 0.5 to 1.0, density times turbulence variable from 0.035 to 2.6.
All inputs are finite; a program needn't handle non-finite values.
Results may differ from the reference program's by a relative error of at most 0.00018.
Values sent between devices are 32-bit elements; how exact they have to be, the bound alone decides.
No kernel may reach another device: no remote copies, remote signals or barrier semaphores. Data moves between devices by JAX's collectives and lax.ppermute only.
A program may use at most 128 MiB of HBM per device.

```python
import math
import jax
import jax.numpy as jnp
from jax import lax

NT = 32
NJ = 128
NK = 8
NI = 512


def draw_state(key, part):
    key = jax.random.fold_in(key, 11)
    keys = jax.random.split(key, 6)
    shape = (NT, NK, NI, NJ)
    density = jax.random.uniform(keys[0], shape, jnp.float32, 0.7, 1.3)
    velocity = [jnp.clip(0.2 * jax.random.normal(keys[1 + index_value], shape, jnp.float32), -0.6, 0.6) for index_value in range(3)]
    pressure = jax.random.uniform(keys[4], shape, jnp.float32, 0.5, 1.0)
    turbulence = 0.05 * jnp.exp(jax.random.uniform(keys[5], shape, jnp.float32, 0.0, math.log(40.0)))
    speed_sq = velocity[0] * velocity[0] + velocity[1] * velocity[1] + velocity[2] * velocity[2]
    energy = pressure / 0.4 + 0.5 * density * speed_sq
    stacked = jnp.stack([density, density * velocity[0], density * velocity[1], density * velocity[2], energy, density * turbulence], axis=1)
    return stacked.astype(jnp.float32)


def block_levels(own_key, extent, cuts, least, high):
    level = 1.0
    for position, parts in cuts:
        heights = jax.random.uniform(jax.random.fold_in(jax.random.fold_in(own_key, 6), position), (parts,), jnp.float32, least / len(cuts), high / len(cuts))
        level = level * jnp.repeat(jnp.exp(heights), extent[position] // parts).reshape((-1,) + (1,) * (len(extent) - 1 - position))
    return level


def normal_values(own_key, dims, deviation, bound, pieces=(), kind=jnp.bfloat16):
    drawn = deviation * jax.random.normal(own_key, dims, jnp.float32)
    if pieces:
        drawn = drawn * block_levels(own_key, dims, pieces, -0.22, 0.18)
    return jnp.clip(drawn, -bound, bound).astype(kind)


def setup_inputs(seed: int = 0) -> dict:
    key_of = jax.random.split(jax.random.key(seed), 4)
    return {
        "state": draw_state(jax.random.fold_in(key_of[3], 71), 0),
        "metrics": normal_values(key_of[1], (3, 3, NK, NI, NJ), 0.7, 3.0, ((3, 16),), jnp.float32),
        "volume": jnp.clip(jnp.exp(math.log(2.0) - 1.3862944 * jax.random.uniform(key_of[2], (NK, NI, NJ), jnp.float32) ** block_levels(key_of[2], (NK, NI, NJ), ((1, 16),), -0.2, 0.2)), 0.5, 2.0),
    }


dissipation = 0.03125
viscosity = 0.2
frequency = 0.25

def spectral_table(table_size):
    index_rows = jnp.arange(table_size, dtype=jnp.int32)
    distance = index_rows[:, None] - index_rows[None, :]
    signs = jnp.where(distance % 2 == 0, 1.0, -1.0).astype(jnp.float32)
    safe = jnp.where(distance == 0, 1, distance).astype(jnp.float32)
    tangent = jnp.tan(math.pi / table_size * safe)
    return jnp.where(distance == 0, 0.0, 0.5 * signs / tangent).astype(jnp.float32)

def take_range(array, first, last, axis_from_end):
    return lax.slice_in_dim(array, first, last, axis=array.ndim + axis_from_end)

def edge_pad(array, width, axis_from_end):
    pad_widths = [(0, 0)] * array.ndim
    pad_widths[array.ndim + axis_from_end] = (width, width)
    return jnp.pad(array, pad_widths, mode='edge')

def state_flux(field, normals):
    density = field[..., 0, :, :, :]
    momentum = field[..., 1:4, :, :, :]
    velocity = momentum / density[..., None, :, :, :]
    normal_speed = lax.optimization_barrier(jnp.sum(velocity * normals, axis=-4))
    pressure = 0.4 * (field[..., 4, :, :, :] - 0.5 * lax.optimization_barrier(jnp.sum(momentum * velocity, axis=-4)))
    sound_speed = jnp.sqrt(1.4 * pressure / density)
    face_area = jnp.sqrt(lax.optimization_barrier(jnp.sum(normals * normals, axis=0)))
    radius = jnp.abs(normal_speed) + sound_speed * face_area
    cell_flux = jnp.concatenate([(density * normal_speed)[..., None, :, :, :], momentum * normal_speed[..., None, :, :, :] + pressure[..., None, :, :, :] * normals, ((field[..., 4, :, :, :] + pressure) * normal_speed)[..., None, :, :, :], (field[..., 5, :, :, :] * normal_speed)[..., None, :, :, :]], axis=-4)
    return (cell_flux, radius)

def direction_residual(padded, metric_padded, axis_from_end):
    length = padded.shape[padded.ndim + axis_from_end] - 4
    inner_cells = take_range(padded, 1, length + 3, axis_from_end)
    cell_flux, radius = state_flux(inner_cells, metric_padded)
    central = 0.5 * (take_range(cell_flux, 0, length + 1, axis_from_end) + take_range(cell_flux, 1, length + 2, axis_from_end))
    radius_face = 0.5 * (take_range(radius, 0, length + 1, axis_from_end) + take_range(radius, 1, length + 2, axis_from_end))
    fourth = take_range(padded, 3, length + 4, axis_from_end) - 3.0 * take_range(padded, 2, length + 3, axis_from_end) + 3.0 * take_range(padded, 1, length + 2, axis_from_end) - take_range(padded, 0, length + 1, axis_from_end)
    face_flux = central - dissipation * radius_face[..., None, :, :, :] * fourth
    return take_range(face_flux, 1, length + 1, axis_from_end) - take_range(face_flux, 0, length, axis_from_end)

def spatial(field, field_wrap, metric_wrap, metrics, volume):
    convective = direction_residual(field_wrap, metric_wrap, -2)
    convective = convective + direction_residual(edge_pad(field, 2, -1), edge_pad(metrics[1], 1, -1), -1)
    convective = convective + direction_residual(edge_pad(field, 2, -3), edge_pad(metrics[2], 1, -3), -3)
    length = field.shape[-1]
    padded_j = edge_pad(field, 1, -1)
    geometry = edge_pad(lax.optimization_barrier(jnp.sum(metrics[1] * metrics[1], axis=0)) / volume, 1, -1)
    coefficient = viscosity * (1.0 + padded_j[..., 5, :, :, :]) * geometry
    face_coef = 0.5 * (take_range(coefficient, 0, length + 1, -1) + take_range(coefficient, 1, length + 2, -1))
    difference = take_range(padded_j, 1, length + 2, -1) - take_range(padded_j, 0, length + 1, -1)
    face_term = face_coef[..., None, :, :, :] * difference
    var_mask = jnp.array([0.0, 1.0, 1.0, 1.0, 1.0, 1.0], jnp.float32)[:, None, None, None]
    viscous = (take_range(face_term, 1, length + 1, -1) - take_range(face_term, 0, length, -1)) * var_mask
    return convective - viscous

def wrap_pad(array, width):
    return jnp.concatenate([array[..., -width:, :], array, array[..., :width, :]], axis=-2)

def reference(state, metrics, volume):
    derivative = spectral_table(NT)
    time_term = jnp.einsum('nm,mvkij->nvkij', derivative, state, precision=lax.Precision.HIGHEST)
    metric_wrap = wrap_pad(metrics[0], 1)

    def per_instance(field):
        return spatial(field, wrap_pad(field, 2), metric_wrap, metrics, volume)
    local_terms = lax.map(per_instance, state)
    return local_terms + frequency * volume * time_term
```

```python
import math

import jax
import jax.numpy as jnp
import numpy as np
from jax import lax
from jax.experimental import pallas as pl
from jax.experimental.pallas import tpu as pltpu
from jax.sharding import PartitionSpec as P

NT = 32
NJ = 128
TILE = 8

dissipation = 0.03125
viscosity = 0.2
frequency = 0.25


def kernel_row(size):
    row = np.zeros(size)
    for k in range(1, size):
        if 2 * k != size:
            row[k] = 0.5 * (-1.0) ** k / math.tan(math.pi * k / size)
    return row


def skew_sums(values, row):
    size = len(values)
    at = lambda n: values[n % size] if (n // size) % 2 == 0 else -values[n % size]
    out = []
    for n in range(size):
        total = None
        for m in range(size):
            k = n - m
            weight = row[k % size] if k >= 0 else -row[k % size]
            if weight == 0.0:
                continue
            term = np.float32(weight) * values[m]
            total = term if total is None else total + term
        out.append(total)
    return out


def circular_sums(values, row):
    size = len(values)
    half = size // 2
    if size == 2:
        return None
    plus = [values[n] + values[n + half] for n in range(half)]
    minus = [values[n] - values[n + half] for n in range(half)]
    even = circular_sums(plus, 0.5 * (row[:half] + row[half:]))
    odd = skew_sums(minus, 0.5 * (row[:half] - row[half:]))
    if even is None:
        return odd + [-value for value in odd]
    return [a + b for a, b in zip(even, odd)] + [a - b for a, b in zip(even, odd)]


def time_kernel(state_ref, out_ref):
    row = frequency * kernel_row(NT)

    def step(tile, carry):
        rows = pl.ds(pl.multiple_of(tile * TILE, TILE), TILE)
        values = [state_ref[n, rows, :] for n in range(NT)]
        for n, value in enumerate(circular_sums(values, row)):
            out_ref[n, rows, :] = value
        return carry

    lax.fori_loop(0, state_ref.shape[1] // TILE, step, 0)


def time_terms(gathered):
    return pl.pallas_call(
        time_kernel,
        out_shape=jax.ShapeDtypeStruct(gathered.shape, jnp.float32),
        in_specs=[pl.BlockSpec(memory_space=pltpu.VMEM)],
        out_specs=pl.BlockSpec(memory_space=pltpu.VMEM),
        compiler_params=pltpu.CompilerParams(vmem_limit_bytes=32 * 2**20),
        cost_estimate=pl.CostEstimate(
            flops=24 * gathered.size, bytes_accessed=8 * gathered.size, transcendentals=0
        ),
    )(gathered)


def primitives(q):
    inverse = 1.0 / q[0]
    speed = [q[1] * inverse, q[2] * inverse, q[3] * inverse]
    pressure = 0.4 * (q[4] - 0.5 * (q[1] * speed[0] + q[2] * speed[1] + q[3] * speed[2]))
    sound = jnp.sqrt(1.4 * pressure * inverse)
    return speed, pressure, sound


def along(speed, sound, normal):
    normal_speed = speed[0] * normal[0] + speed[1] * normal[1] + speed[2] * normal[2]
    area = jnp.sqrt(normal[0] * normal[0] + normal[1] * normal[1] + normal[2] * normal[2])
    return normal_speed, jnp.abs(normal_speed) + sound * area


def flux(v, q, normal_speed, pressure, normal):
    if v in (1, 2, 3):
        return q * normal_speed + pressure * normal[v - 1]
    if v == 4:
        return (q + pressure) * normal_speed
    return q * normal_speed


def spatial_kernel(
    state_ref, halo_ref, metric_ref, metric_halo_ref, volume_ref, time_ref, out_ref, prim_ref, span_ref
):
    depth, height, width = state_ref.shape[2:]
    lane = lax.broadcasted_iota(jnp.int32, (height, width), 1)
    first = lane == 0
    last = lane == width - 1
    back = lambda x: pltpu.roll(x, 1, 1)
    ahead = lambda x: pltpu.roll(x, width - 1, 1)
    rows = height + TILE
    down = lambda x: pltpu.roll(x, 1, 0)
    up = lambda x: pltpu.roll(x, rows - 1, 0)

    def prepare(k, carry):
        q = [state_ref[0, v, k] for v in range(6)]
        speed, pressure, sound = primitives(q)
        for v in range(3):
            prim_ref[v, k] = speed[v]
        prim_ref[3, k] = pressure
        prim_ref[4, k] = sound
        normal = [metric_ref[2, c, k] for c in range(3)]
        normal_speed, radius = along(speed, sound, normal)
        span_ref[6, k] = radius
        for v in range(6):
            span_ref[v, k] = flux(v, q[v], normal_speed, pressure, normal)
        return carry

    lax.fori_loop(0, depth, prepare, 0)

    def step(k, carry):
        speed = [prim_ref[v, k] for v in range(3)]
        pressure = prim_ref[3, k]
        sound = prim_ref[4, k]
        halo = [halo_ref[0, v, k] for v in range(6)]
        halo_speed, halo_pressure, halo_sound = primitives(halo)
        join = lambda a, b: jnp.concatenate([a, b], axis=0)
        wrap_normal = [join(metric_ref[0, c, k], metric_halo_ref[c, k]) for c in range(3)]
        wrap_pressure = join(pressure, halo_pressure)
        wrap_speed, wrap_radius = along(
            [join(a, b) for a, b in zip(speed, halo_speed)], join(sound, halo_sound), wrap_normal
        )
        wrap_weight = dissipation * (wrap_radius + down(wrap_radius))
        wall_normal = [metric_ref[1, c, k] for c in range(3)]
        wall_speed, wall_radius = along(speed, sound, wall_normal)
        wall_weight = dissipation * (wall_radius + jnp.where(first, wall_radius, back(wall_radius)))
        wall_end = (2.0 * dissipation) * wall_radius
        volume = volume_ref[k]
        squared = (
            wall_normal[0] * wall_normal[0] + wall_normal[1] * wall_normal[1] + wall_normal[2] * wall_normal[2]
        )
        coefficient = viscosity * (1.0 + state_ref[0, 5, k]) * (squared / volume)
        coefficient = coefficient + back(coefficient)
        k1 = jnp.maximum(k - 1, 0)
        k2 = jnp.maximum(k - 2, 0)
        k3 = jnp.minimum(k + 1, depth - 1)
        k4 = jnp.minimum(k + 2, depth - 1)
        span_low = dissipation * (span_ref[6, k] + span_ref[6, k1])
        span_high = dissipation * (span_ref[6, k] + span_ref[6, k3])

        for v in range(6):
            q = state_ref[0, v, k]
            cells = join(q, halo[v])
            face = flux(v, cells, wrap_speed, wrap_pressure, wrap_normal)
            step_one = cells - down(cells)
            step_two = up(step_one) - step_one
            step_three = step_two - down(step_two)
            face = face + down(face) - wrap_weight * step_three
            total = (up(face) - face)[:height]
            cell = flux(v, q, wall_speed, pressure, wall_normal)
            step_one = jnp.where(first, 0.0, q - back(q))
            step_two = ahead(step_one) - step_one
            step_three = step_two - jnp.where(first, 0.0, back(step_two))
            face = cell + jnp.where(first, cell, back(cell)) - wall_weight * step_three
            if v > 0:
                face = face - coefficient * step_one
            end = 2.0 * cell - wall_end * step_one
            total = total + (jnp.where(last, end, ahead(face)) - face)
            q1 = state_ref[0, v, k1]
            q2 = state_ref[0, v, k2]
            q3 = state_ref[0, v, k3]
            q4 = state_ref[0, v, k4]
            total = total + (span_ref[v, k3] - span_ref[v, k1])
            total = total - span_high * (q4 - q1 - 3.0 * (q3 - q))
            total = total + span_low * (q3 - q2 - 3.0 * (q - q1))
            term = jnp.concatenate([time_ref[2 * k, 0, v], time_ref[2 * k + 1, 0, v]], axis=0)
            out_ref[0, v, k] = 0.5 * total + volume * term
        return carry

    lax.fori_loop(0, depth, step, 0)


def residual_of(state, halo, metrics, metric_halo, volume, time_term):
    count, variables, depth, height, width = state.shape
    owners = time_term.shape[0]
    whole = lambda a: pl.BlockSpec(a.shape, lambda n: (0,) * a.ndim)
    each = lambda a: pl.BlockSpec((1,) + a.shape[1:], lambda n: (n,) + (0,) * (a.ndim - 1))
    return pl.pallas_call(
        spatial_kernel,
        grid=(count,),
        out_shape=jax.ShapeDtypeStruct(state.shape, jnp.float32),
        in_specs=[
            each(state),
            each(halo),
            whole(metrics),
            whole(metric_halo),
            whole(volume),
            pl.BlockSpec((owners, 1) + time_term.shape[2:], lambda n: (0, n, 0, 0, 0)),
        ],
        out_specs=each(state),
        scratch_shapes=[
            pltpu.VMEM((5, depth, height, width), jnp.float32),
            pltpu.VMEM((7, depth, height, width), jnp.float32),
        ],
        compiler_params=pltpu.CompilerParams(vmem_limit_bytes=48 * 2**20),
        cost_estimate=pl.CostEstimate(
            flops=400 * count * depth * height * width,
            bytes_accessed=12 * state.size + 4 * metrics.size,
            transcendentals=0,
        ),
    )(state, halo, metrics, metric_halo, volume, time_term)


def wrap_halos(state, metrics):
    count = lax.axis_size("wrap")
    onward = [(i, (i + 1) % count) for i in range(count)]
    backward = [((i + 1) % count, i) for i in range(count)]
    inst_count, variables, depth, height, width = state.shape
    pack = lambda cells, face: jnp.concatenate(
        [cells.reshape(-1, width), face.reshape(-1, width)], axis=0
    )
    size = inst_count * variables * depth * 2
    before = lax.ppermute(pack(state[..., -2:, :], metrics[0, :, :, -1:]), "wrap", onward)
    after = lax.ppermute(pack(state[..., :2, :], metrics[0, :, :, :1]), "wrap", backward)
    cells = lambda packed: packed[:size].reshape(inst_count, variables, depth, 2, width)
    face = lambda packed: packed[size:].reshape(3, depth, 1, width)
    halo = jnp.concatenate([cells(after), cells(after), cells(before), cells(before)], axis=-2)
    metric_halo = jnp.concatenate([face(after)] * 4 + [face(before)] * 4, axis=-2)
    return halo, metric_halo


def body(state, metrics, volume):
    inst_count, variables, depth, height, width = state.shape
    owners = lax.axis_size("inst")
    parts = owners // depth
    lines = height // parts
    halo, metric_halo = wrap_halos(state, metrics)
    sent = state.reshape(inst_count, variables, depth, parts, lines, width)
    sent = sent.transpose(2, 3, 0, 1, 4, 5).reshape(owners, inst_count * variables * lines, width)
    held = lax.all_to_all(sent, "inst", 0, 0, tiled=True)
    held = held.reshape(owners * inst_count, variables * lines, width)
    terms = time_terms(held).reshape(owners, inst_count * variables * lines, width)
    terms = lax.all_to_all(terms, "inst", 0, 0, tiled=True)
    terms = terms.reshape(owners, inst_count, variables, lines, width)
    return residual_of(state, halo, metrics, metric_halo, volume, terms)


def solution(mesh):
    in_specs = (
        P("inst", None, None, "wrap", None),
        P(None, None, None, "wrap", None),
        P(None, "wrap", None),
    )
    out_specs = P("inst", None, None, "wrap", None)
    return jax.shard_map(body, mesh=mesh, in_specs=in_specs, out_specs=out_specs, check_vma=False)
```

```python
import functools
import math

import jax
import jax.numpy as jnp
import numpy as np
from jax import lax
from jax.experimental import pallas as pl
from jax.experimental.pallas import tpu as pltpu
from jax.sharding import PartitionSpec as P

NT = 32
NJ = 128
TILE = 8

dissipation = 0.03125
viscosity = 0.2
frequency = 0.25
GROUPS = (6,)


def kernel_row(size):
    row = np.zeros(size)
    for k in range(1, size):
        if 2 * k != size:
            row[k] = 0.5 * (-1.0) ** k / math.tan(math.pi * k / size)
    return row


def skew_sums(values, row):
    size = len(values)
    at = lambda n: values[n % size] if (n // size) % 2 == 0 else -values[n % size]
    out = []
    for n in range(size):
        total = None
        for m in range(size):
            k = n - m
            weight = row[k % size] if k >= 0 else -row[k % size]
            if weight == 0.0:
                continue
            term = np.float32(weight) * values[m]
            total = term if total is None else total + term
        out.append(total)
    return out


def circular_sums(values, row):
    size = len(values)
    half = size // 2
    if size == 2:
        return None
    plus = [values[n] + values[n + half] for n in range(half)]
    minus = [values[n] - values[n + half] for n in range(half)]
    even = circular_sums(plus, 0.5 * (row[:half] + row[half:]))
    odd = skew_sums(minus, 0.5 * (row[:half] - row[half:]))
    if even is None:
        return odd + [-value for value in odd]
    return [a + b for a, b in zip(even, odd)] + [a - b for a, b in zip(even, odd)]


def time_kernel(state_ref, out_ref):
    row = frequency * kernel_row(NT)

    def step(tile, carry):
        rows = pl.ds(pl.multiple_of(tile * TILE, TILE), TILE)
        values = [state_ref[n, rows, :] for n in range(NT)]
        for n, value in enumerate(circular_sums(values, row)):
            out_ref[n, rows, :] = value
        return carry

    lax.fori_loop(0, state_ref.shape[1] // TILE, step, 0)


def time_terms(gathered):
    return pl.pallas_call(
        time_kernel,
        out_shape=jax.ShapeDtypeStruct(gathered.shape, jnp.float32),
        in_specs=[pl.BlockSpec(memory_space=pltpu.VMEM)],
        out_specs=pl.BlockSpec(memory_space=pltpu.VMEM),
        compiler_params=pltpu.CompilerParams(vmem_limit_bytes=32 * 2**20),
        cost_estimate=pl.CostEstimate(
            flops=24 * gathered.size, bytes_accessed=8 * gathered.size, transcendentals=0
        ),
    )(gathered)


def primitives(q):
    inverse = 1.0 / q[0]
    speed = [q[1] * inverse, q[2] * inverse, q[3] * inverse]
    pressure = 0.4 * (q[4] - 0.5 * (q[1] * speed[0] + q[2] * speed[1] + q[3] * speed[2]))
    sound = jnp.sqrt(1.4 * pressure * inverse)
    return speed, pressure, sound


def along(speed, sound, normal):
    normal_speed = speed[0] * normal[0] + speed[1] * normal[1] + speed[2] * normal[2]
    area = jnp.sqrt(normal[0] * normal[0] + normal[1] * normal[1] + normal[2] * normal[2])
    return normal_speed, jnp.abs(normal_speed) + sound * area


def flux(v, q, normal_speed, pressure, normal):
    if v in (1, 2, 3):
        return q * normal_speed + pressure * normal[v - 1]
    if v == 4:
        return (q + pressure) * normal_speed
    return q * normal_speed


def spatial_kernel(
    state_ref, halo_ref, metric_ref, metric_halo_ref, volume_ref, out_ref, prim_ref, span_ref
):
    depth, height, width = state_ref.shape[2:]
    lane = lax.broadcasted_iota(jnp.int32, (height, width), 1)
    first = lane == 0
    last = lane == width - 1
    back = lambda x: pltpu.roll(x, 1, 1)
    ahead = lambda x: pltpu.roll(x, width - 1, 1)
    rows = height + TILE
    down = lambda x: pltpu.roll(x, 1, 0)
    up = lambda x: pltpu.roll(x, rows - 1, 0)

    def prepare(k, carry):
        q = [state_ref[0, v, k] for v in range(6)]
        speed, pressure, sound = primitives(q)
        for v in range(3):
            prim_ref[v, k] = speed[v]
        prim_ref[3, k] = pressure
        prim_ref[4, k] = sound
        normal = [metric_ref[2, c, k] for c in range(3)]
        normal_speed, radius = along(speed, sound, normal)
        span_ref[6, k] = radius
        for v in range(6):
            span_ref[v, k] = flux(v, q[v], normal_speed, pressure, normal)
        return carry

    lax.fori_loop(0, depth, prepare, 0)

    def step(k, carry):
        speed = [prim_ref[v, k] for v in range(3)]
        pressure = prim_ref[3, k]
        sound = prim_ref[4, k]
        halo = [halo_ref[0, v, k] for v in range(6)]
        halo_speed, halo_pressure, halo_sound = primitives(halo)
        join = lambda a, b: jnp.concatenate([a, b], axis=0)
        wrap_normal = [join(metric_ref[0, c, k], metric_halo_ref[c, k]) for c in range(3)]
        wrap_pressure = join(pressure, halo_pressure)
        wrap_speed, wrap_radius = along(
            [join(a, b) for a, b in zip(speed, halo_speed)], join(sound, halo_sound), wrap_normal
        )
        wrap_weight = dissipation * (wrap_radius + down(wrap_radius))
        wall_normal = [metric_ref[1, c, k] for c in range(3)]
        wall_speed, wall_radius = along(speed, sound, wall_normal)
        wall_weight = dissipation * (wall_radius + jnp.where(first, wall_radius, back(wall_radius)))
        wall_end = (2.0 * dissipation) * wall_radius
        volume = volume_ref[k]
        squared = (
            wall_normal[0] * wall_normal[0] + wall_normal[1] * wall_normal[1] + wall_normal[2] * wall_normal[2]
        )
        coefficient = viscosity * (1.0 + state_ref[0, 5, k]) * (squared / volume)
        coefficient = coefficient + back(coefficient)
        k1 = jnp.maximum(k - 1, 0)
        k2 = jnp.maximum(k - 2, 0)
        k3 = jnp.minimum(k + 1, depth - 1)
        k4 = jnp.minimum(k + 2, depth - 1)
        span_low = dissipation * (span_ref[6, k] + span_ref[6, k1])
        span_high = dissipation * (span_ref[6, k] + span_ref[6, k3])

        for v in range(6):
            q = state_ref[0, v, k]
            cells = join(q, halo[v])
            face = flux(v, cells, wrap_speed, wrap_pressure, wrap_normal)
            step_one = cells - down(cells)
            step_two = up(step_one) - step_one
            step_three = step_two - down(step_two)
            face = face + down(face) - wrap_weight * step_three
            total = (up(face) - face)[:height]
            cell = flux(v, q, wall_speed, pressure, wall_normal)
            step_one = jnp.where(first, 0.0, q - back(q))
            step_two = ahead(step_one) - step_one
            step_three = step_two - jnp.where(first, 0.0, back(step_two))
            face = cell + jnp.where(first, cell, back(cell)) - wall_weight * step_three
            if v > 0:
                face = face - coefficient * step_one
            end = 2.0 * cell - wall_end * step_one
            total = total + (jnp.where(last, end, ahead(face)) - face)
            q1 = state_ref[0, v, k1]
            q2 = state_ref[0, v, k2]
            q3 = state_ref[0, v, k3]
            q4 = state_ref[0, v, k4]
            total = total + (span_ref[v, k3] - span_ref[v, k1])
            total = total - span_high * (q4 - q1 - 3.0 * (q3 - q))
            total = total + span_low * (q3 - q2 - 3.0 * (q - q1))
            out_ref[0, v, k] = 0.5 * total
        return carry

    lax.fori_loop(0, depth, step, 0)


def spatial(state, halo, metrics, metric_halo, volume):
    count, variables, depth, height, width = state.shape
    whole = lambda a: pl.BlockSpec(a.shape, lambda n: (0,) * a.ndim)
    each = lambda a: pl.BlockSpec((1,) + a.shape[1:], lambda n: (n,) + (0,) * (a.ndim - 1))
    return pl.pallas_call(
        spatial_kernel,
        grid=(count,),
        out_shape=jax.ShapeDtypeStruct(state.shape, jnp.float32),
        in_specs=[
            each(state),
            each(halo),
            whole(metrics),
            whole(metric_halo),
            whole(volume),
        ],
        out_specs=each(state),
        scratch_shapes=[
            pltpu.VMEM((5, depth, height, width), jnp.float32),
            pltpu.VMEM((7, depth, height, width), jnp.float32),
        ],
        compiler_params=pltpu.CompilerParams(vmem_limit_bytes=48 * 2**20),
        cost_estimate=pl.CostEstimate(
            flops=400 * count * depth * height * width,
            bytes_accessed=12 * state.size + 4 * metrics.size,
            transcendentals=0,
        ),
    )(state, halo, metrics, metric_halo, volume)


def combine_kernel(groups, spatial_ref, volume_ref, *refs):
    out_ref = refs[-1]
    depth = spatial_ref.shape[2]
    parts = refs[0].shape[0] // depth

    def step(k, carry):
        volume = volume_ref[k]
        v = 0
        for ref, count in zip(refs, groups):
            for w in range(count):
                term = jnp.concatenate([ref[parts * k + p, 0, w] for p in range(parts)], axis=0)
                out_ref[0, v, k] = spatial_ref[0, v, k] + volume * term
                v += 1
        return carry

    lax.fori_loop(0, depth, step, 0)


def combined(local, volume, terms):
    whole = lambda a: pl.BlockSpec(a.shape, lambda n: (0,) * a.ndim)
    each = lambda a: pl.BlockSpec((1,) + a.shape[1:], lambda n: (n,) + (0,) * (a.ndim - 1))
    owned = lambda a: pl.BlockSpec((a.shape[0], 1) + a.shape[2:], lambda n: (0, n, 0, 0, 0))
    return pl.pallas_call(
        functools.partial(combine_kernel, [term.shape[2] for term in terms]),
        grid=(local.shape[0],),
        out_shape=jax.ShapeDtypeStruct(local.shape, jnp.float32),
        in_specs=[each(local), whole(volume)] + [owned(term) for term in terms],
        out_specs=each(local),
        compiler_params=pltpu.CompilerParams(vmem_limit_bytes=32 * 2**20),
        cost_estimate=pl.CostEstimate(
            flops=2 * local.size, bytes_accessed=12 * local.size, transcendentals=0
        ),
    )(local, volume, *terms)


def wrap_halos(state, metrics):
    count = lax.axis_size("wrap")
    onward = [(i, (i + 1) % count) for i in range(count)]
    backward = [((i + 1) % count, i) for i in range(count)]
    inst_count, variables, depth, height, width = state.shape
    pack = lambda cells, face: jnp.concatenate(
        [cells.reshape(-1, width), face.reshape(-1, width)], axis=0
    )
    size = inst_count * variables * depth * 2
    before = lax.ppermute(pack(state[..., -2:, :], metrics[0, :, :, -1:]), "wrap", onward)
    after = lax.ppermute(pack(state[..., :2, :], metrics[0, :, :, :1]), "wrap", backward)
    cells = lambda packed: packed[:size].reshape(inst_count, variables, depth, 2, width)
    face = lambda packed: packed[size:].reshape(3, depth, 1, width)
    halo = jnp.concatenate([cells(after), cells(after), cells(before), cells(before)], axis=-2)
    metric_halo = jnp.concatenate([face(after)] * 4 + [face(before)] * 4, axis=-2)
    return halo, metric_halo


def body(state, metrics, volume):
    inst_count, variables, depth, height, width = state.shape
    owners = lax.axis_size("inst")
    parts = owners // depth
    lines = height // parts
    halo, metric_halo = wrap_halos(state, metrics)
    split = state.reshape(inst_count, variables, depth, parts, lines, width)
    held = []
    first = 0
    for count in GROUPS:
        sent = split[:, first : first + count].transpose(2, 3, 0, 1, 4, 5)
        sent = sent.reshape(owners, inst_count * count * lines, width)
        held.append(lax.all_to_all(sent, "inst", 0, 0, tiled=True))
        first += count
    local = spatial(state, halo, metrics, metric_halo, volume)
    terms = []
    for part, count in zip(held, GROUPS):
        part = time_terms(part.reshape(owners * inst_count, count * lines, width))
        part = part.reshape(owners, inst_count * count * lines, width)
        part = lax.all_to_all(part, "inst", 0, 0, tiled=True)
        terms.append(part.reshape(owners, inst_count, count, lines, width))
    return combined(local, volume, terms)


def solution(mesh):
    in_specs = (
        P("inst", None, None, "wrap", None),
        P(None, None, None, "wrap", None),
        P(None, "wrap", None),
    )
    out_specs = P("inst", None, None, "wrap", None)
    return jax.shard_map(body, mesh=mesh, in_specs=in_specs, out_specs=out_specs, check_vma=False)
```

```python
import math

import jax
import jax.numpy as jnp
import numpy as np
from jax import lax
from jax.experimental import pallas as pl
from jax.experimental.pallas import tpu as pltpu
from jax.sharding import PartitionSpec as P

NT = 32
NJ = 128
TILE = 8
BLOCKS = 2

dissipation = 0.03125
viscosity = 0.2
frequency = 0.25


def kernel_row(size):
    row = np.zeros(size)
    for k in range(1, size):
        if 2 * k != size:
            row[k] = 0.5 * (-1.0) ** k / math.tan(math.pi * k / size)
    return row


def weighted(pairs):
    total = None
    for weight, value in pairs:
        if abs(weight) > 1e-12:
            term = np.float32(weight) * value
            total = term if total is None else total + term
    return total


def skew_sums(values, row):
    size = len(values)
    half = size // 2
    if size == 2:
        return [-np.float32(row[1]) * values[1], np.float32(row[1]) * values[0]]
    at = lambda k: row[k % size] * (1.0 if (k // size) % 2 == 0 else -1.0)
    even = [values[0]] + [values[m] - values[size - m] for m in range(1, half)]
    odd = [None] + [values[m] + values[size - m] for m in range(1, half)] + [values[half]]
    from_even = [None] + [
        weighted(
            [(at(n), even[0])] + [(0.5 * (at(n - m) + at(n + m)), even[m]) for m in range(1, half)]
        )
        for n in range(1, half + 1)
    ]
    from_odd = [
        weighted(
            [(0.5 * (at(n - m) - at(n + m)), odd[m]) for m in range(1, half)] + [(at(n - half), odd[half])]
        )
        for n in range(half)
    ]
    out = [from_odd[0]] + [from_odd[n] + from_even[n] for n in range(1, half)] + [from_even[half]]
    return out + [from_even[n] - from_odd[n] for n in range(half - 1, 0, -1)]


def circular_sums(values, row):
    size = len(values)
    half = size // 2
    if size == 2:
        return None
    plus = [values[n] + values[n + half] for n in range(half)]
    minus = [values[n] - values[n + half] for n in range(half)]
    even = circular_sums(plus, 0.5 * (row[:half] + row[half:]))
    odd = skew_sums(minus, 0.5 * (row[:half] - row[half:]))
    if even is None:
        return odd + [-value for value in odd]
    return [a + b for a, b in zip(even, odd)] + [a - b for a, b in zip(even, odd)]


def time_kernel(state_ref, out_ref):
    row = frequency * kernel_row(NT)

    def step(tile, carry):
        rows = pl.ds(pl.multiple_of(tile * TILE, TILE), TILE)
        values = [state_ref[n, rows, :] for n in range(NT)]
        for n, value in enumerate(circular_sums(values, row)):
            out_ref[n, rows, :] = value
        return carry

    lax.fori_loop(0, state_ref.shape[1] // TILE, step, 0)


def time_terms(gathered):
    return pl.pallas_call(
        time_kernel,
        out_shape=jax.ShapeDtypeStruct(gathered.shape, jnp.float32),
        in_specs=[pl.BlockSpec(memory_space=pltpu.VMEM)],
        out_specs=pl.BlockSpec(memory_space=pltpu.VMEM),
        compiler_params=pltpu.CompilerParams(vmem_limit_bytes=16 * 2**20),
        cost_estimate=pl.CostEstimate(
            flops=16 * gathered.size, bytes_accessed=8 * gathered.size, transcendentals=0
        ),
    )(gathered)


def primitives(q):
    inverse = 1.0 / q[0]
    speed = [q[1] * inverse, q[2] * inverse, q[3] * inverse]
    pressure = 0.4 * (q[4] - 0.5 * (q[1] * speed[0] + q[2] * speed[1] + q[3] * speed[2]))
    sound = jnp.sqrt(1.4 * pressure * inverse)
    return speed, pressure, sound


def along(speed, sound, normal):
    normal_speed = speed[0] * normal[0] + speed[1] * normal[1] + speed[2] * normal[2]
    area = jnp.sqrt(normal[0] * normal[0] + normal[1] * normal[1] + normal[2] * normal[2])
    return normal_speed, jnp.abs(normal_speed) + sound * area


def flux(v, q, normal_speed, pressure, normal):
    if v in (1, 2, 3):
        return q * normal_speed + pressure * normal[v - 1]
    if v == 4:
        return (q + pressure) * normal_speed
    return q * normal_speed


def spatial_kernel(
    state_ref, halo_ref, metric_ref, metric_halo_ref, volume_ref, out_ref, prim_ref, span_ref
):
    depth, height, width = state_ref.shape[2:]
    lane = lax.broadcasted_iota(jnp.int32, (height, width), 1)
    first = lane == 0
    last = lane == width - 1
    back = lambda x: pltpu.roll(x, 1, 1)
    ahead = lambda x: pltpu.roll(x, width - 1, 1)
    rows = height + TILE
    down = lambda x: pltpu.roll(x, 1, 0)
    up = lambda x: pltpu.roll(x, rows - 1, 0)

    def prepare(k, carry):
        q = [state_ref[0, v, k] for v in range(6)]
        speed, pressure, sound = primitives(q)
        for v in range(3):
            prim_ref[v, k] = speed[v]
        prim_ref[3, k] = pressure
        prim_ref[4, k] = sound
        normal = [metric_ref[2, c, k] for c in range(3)]
        normal_speed, radius = along(speed, sound, normal)
        span_ref[6, k] = radius
        for v in range(6):
            span_ref[v, k] = flux(v, q[v], normal_speed, pressure, normal)
        return carry

    lax.fori_loop(0, depth, prepare, 0)

    def step(k, carry):
        speed = [prim_ref[v, k] for v in range(3)]
        pressure = prim_ref[3, k]
        sound = prim_ref[4, k]
        halo = [halo_ref[0, v, k] for v in range(6)]
        halo_speed, halo_pressure, halo_sound = primitives(halo)
        join = lambda a, b: jnp.concatenate([a, b], axis=0)
        wrap_normal = [join(metric_ref[0, c, k], metric_halo_ref[c, k]) for c in range(3)]
        wrap_pressure = join(pressure, halo_pressure)
        wrap_speed, wrap_radius = along(
            [join(a, b) for a, b in zip(speed, halo_speed)], join(sound, halo_sound), wrap_normal
        )
        wrap_weight = dissipation * (wrap_radius + down(wrap_radius))
        wall_normal = [metric_ref[1, c, k] for c in range(3)]
        wall_speed, wall_radius = along(speed, sound, wall_normal)
        wall_weight = dissipation * (wall_radius + jnp.where(first, wall_radius, back(wall_radius)))
        wall_end = (2.0 * dissipation) * wall_radius
        volume = volume_ref[k]
        squared = (
            wall_normal[0] * wall_normal[0] + wall_normal[1] * wall_normal[1] + wall_normal[2] * wall_normal[2]
        )
        coefficient = viscosity * (1.0 + state_ref[0, 5, k]) * (squared / volume)
        coefficient = coefficient + back(coefficient)
        k1 = jnp.maximum(k - 1, 0)
        k2 = jnp.maximum(k - 2, 0)
        k3 = jnp.minimum(k + 1, depth - 1)
        k4 = jnp.minimum(k + 2, depth - 1)
        span_low = dissipation * (span_ref[6, k] + span_ref[6, k1])
        span_high = dissipation * (span_ref[6, k] + span_ref[6, k3])

        for v in range(6):
            q = state_ref[0, v, k]
            cells = join(q, halo[v])
            face = flux(v, cells, wrap_speed, wrap_pressure, wrap_normal)
            step_one = cells - down(cells)
            step_two = up(step_one) - step_one
            step_three = step_two - down(step_two)
            face = face + down(face) - wrap_weight * step_three
            total = (up(face) - face)[:height]
            cell = flux(v, q, wall_speed, pressure, wall_normal)
            step_one = jnp.where(first, 0.0, q - back(q))
            step_two = ahead(step_one) - step_one
            step_three = step_two - jnp.where(first, 0.0, back(step_two))
            face = cell + jnp.where(first, cell, back(cell)) - wall_weight * step_three
            if v > 0:
                face = face - coefficient * step_one
            end = 2.0 * cell - wall_end * step_one
            total = total + (jnp.where(last, end, ahead(face)) - face)
            q1 = state_ref[0, v, k1]
            q2 = state_ref[0, v, k2]
            q3 = state_ref[0, v, k3]
            q4 = state_ref[0, v, k4]
            total = total + (span_ref[v, k3] - span_ref[v, k1])
            total = total - span_high * (q4 - q1 - 3.0 * (q3 - q))
            total = total + span_low * (q3 - q2 - 3.0 * (q - q1))
            out_ref[0, v, k] = 0.5 * total
        return carry

    lax.fori_loop(0, depth, step, 0)


def spatial(state, halo, metrics, metric_halo, volume):
    count, variables, depth, height, width = state.shape
    whole = lambda a: pl.BlockSpec(a.shape, lambda n: (0,) * a.ndim)
    each = lambda a: pl.BlockSpec((1,) + a.shape[1:], lambda n: (n,) + (0,) * (a.ndim - 1))
    return pl.pallas_call(
        spatial_kernel,
        grid=(count,),
        out_shape=jax.ShapeDtypeStruct(state.shape, jnp.float32),
        in_specs=[
            each(state),
            each(halo),
            whole(metrics),
            whole(metric_halo),
            whole(volume),
        ],
        out_specs=each(state),
        scratch_shapes=[
            pltpu.VMEM((5, depth, height, width), jnp.float32),
            pltpu.VMEM((7, depth, height, width), jnp.float32),
        ],
        compiler_params=pltpu.CompilerParams(vmem_limit_bytes=16 * 2**20),
        cost_estimate=pl.CostEstimate(
            flops=400 * count * depth * height * width,
            bytes_accessed=12 * state.size + 4 * metrics.size,
            transcendentals=0,
        ),
    )(state, halo, metrics, metric_halo, volume)


def combine_kernel(spatial_ref, volume_ref, term_ref, out_ref, held_ref, in_sems, out_sems):
    count, variables, depth = spatial_ref.shape[:3]
    parts = term_ref.shape[0] // depth
    run = variables // BLOCKS
    blocks = [(n, slice(b * run, (b + 1) * run)) for n in range(count) for b in range(BLOCKS)]
    fetches = [
        pltpu.make_async_copy(spatial_ref.at[n, r], held_ref.at[n, r], in_sems.at[b])
        for b, (n, r) in enumerate(blocks)
    ]
    writes = [
        pltpu.make_async_copy(held_ref.at[n, r], out_ref.at[n, r], out_sems.at[b])
        for b, (n, r) in enumerate(blocks)
    ]
    for fetch in fetches:
        fetch.start()
    for b, (n, r) in enumerate(blocks):
        fetches[b].wait()

        def step(k, carry):
            volume = volume_ref[k]
            for v in range(r.start, r.stop):
                term = jnp.concatenate([term_ref[parts * k + p, n, v] for p in range(parts)], axis=0)
                held_ref[n, v, k] = held_ref[n, v, k] + volume * term
            return carry

        lax.fori_loop(0, depth, step, 0)
        writes[b].start()
    for write in writes:
        write.wait()


def combined(local, volume, terms):
    count = local.shape[0] * BLOCKS
    vmem = pl.BlockSpec(memory_space=pltpu.VMEM)
    anywhere = pl.BlockSpec(memory_space=pl.ANY)
    return pl.pallas_call(
        combine_kernel,
        out_shape=jax.ShapeDtypeStruct(local.shape, jnp.float32),
        in_specs=[anywhere, vmem, vmem],
        out_specs=anywhere,
        input_output_aliases={0: 0},
        scratch_shapes=[
            pltpu.VMEM(local.shape, jnp.float32),
            pltpu.SemaphoreType.DMA((count,)),
            pltpu.SemaphoreType.DMA((count,)),
        ],
        compiler_params=pltpu.CompilerParams(vmem_limit_bytes=16 * 2**20),
        cost_estimate=pl.CostEstimate(
            flops=2 * local.size, bytes_accessed=12 * local.size, transcendentals=0
        ),
    )(local, volume, terms)


def wrap_halos(state, metrics):
    count = lax.axis_size("wrap")
    onward = [(i, (i + 1) % count) for i in range(count)]
    backward = [((i + 1) % count, i) for i in range(count)]
    inst_count, variables, depth, height, width = state.shape
    pack = lambda cells, face: jnp.concatenate(
        [cells.reshape(-1, width), face.reshape(-1, width)], axis=0
    )
    size = inst_count * variables * depth * 2
    before = lax.ppermute(pack(state[..., -2:, :], metrics[0, :, :, -1:]), "wrap", onward)
    after = lax.ppermute(pack(state[..., :2, :], metrics[0, :, :, :1]), "wrap", backward)
    cells = lambda packed: packed[:size].reshape(inst_count, variables, depth, 2, width)
    face = lambda packed: packed[size:].reshape(3, depth, 1, width)
    halo = jnp.concatenate([cells(after), cells(after), cells(before), cells(before)], axis=-2)
    metric_halo = jnp.concatenate([face(after)] * 4 + [face(before)] * 4, axis=-2)
    return halo, metric_halo


def body(state, metrics, volume):
    inst_count, variables, depth, height, width = state.shape
    owners = lax.axis_size("inst")
    parts = owners // depth
    lines = height // parts
    halo, metric_halo = wrap_halos(state, metrics)
    split = state.reshape(inst_count, variables, depth, parts, lines, width)
    sent = split.transpose(2, 3, 0, 1, 4, 5).reshape(owners, inst_count * variables * lines, width)
    held = lax.all_to_all(sent, "inst", 0, 0, tiled=True)
    terms = time_terms(held.reshape(owners * inst_count, variables * lines, width))
    terms = lax.all_to_all(terms.reshape(sent.shape), "inst", 0, 0, tiled=True)
    terms = terms.reshape(owners, inst_count, variables, lines, width)
    local = spatial(state, halo, metrics, metric_halo, volume)
    return combined(local, volume, terms)


def solution(mesh):
    in_specs = (
        P("inst", None, None, "wrap", None),
        P(None, None, None, "wrap", None),
        P(None, "wrap", None),
    )
    out_specs = P("inst", None, None, "wrap", None)
    return jax.shard_map(body, mesh=mesh, in_specs=in_specs, out_specs=out_specs, check_vma=False)
```

```python
import math

import jax
import jax.numpy as jnp
import numpy as np
from jax import lax
from jax.experimental import pallas as pl
from jax.experimental.pallas import tpu as pltpu
from jax.sharding import PartitionSpec as P

NT = 32
NJ = 128
TILE = 8
WRITES = 4
BLOCKS = 2

dissipation = 0.03125
viscosity = 0.2
frequency = 0.25


def kernel_row(size):
    row = np.zeros(size)
    for k in range(1, size):
        if 2 * k != size:
            row[k] = 0.5 * (-1.0) ** k / math.tan(math.pi * k / size)
    return row


def weighted(pairs):
    total = None
    for weight, value in pairs:
        if abs(weight) > 1e-12:
            term = np.float32(weight) * value
            total = term if total is None else total + term
    return total


def skew_sums(values, row):
    size = len(values)
    half = size // 2
    if size == 2:
        return [-np.float32(row[1]) * values[1], np.float32(row[1]) * values[0]]
    at = lambda k: row[k % size] * (1.0 if (k // size) % 2 == 0 else -1.0)
    even = [values[0]] + [values[m] - values[size - m] for m in range(1, half)]
    odd = [None] + [values[m] + values[size - m] for m in range(1, half)] + [values[half]]
    from_even = [None] + [
        weighted(
            [(at(n), even[0])] + [(0.5 * (at(n - m) + at(n + m)), even[m]) for m in range(1, half)]
        )
        for n in range(1, half + 1)
    ]
    from_odd = [
        weighted(
            [(0.5 * (at(n - m) - at(n + m)), odd[m]) for m in range(1, half)] + [(at(n - half), odd[half])]
        )
        for n in range(half)
    ]
    out = [from_odd[0]] + [from_odd[n] + from_even[n] for n in range(1, half)] + [from_even[half]]
    return out + [from_even[n] - from_odd[n] for n in range(half - 1, 0, -1)]


def circular_sums(values, row):
    size = len(values)
    half = size // 2
    if size == 2:
        return None
    plus = [values[n] + values[n + half] for n in range(half)]
    minus = [values[n] - values[n + half] for n in range(half)]
    even = circular_sums(plus, 0.5 * (row[:half] + row[half:]))
    odd = skew_sums(minus, 0.5 * (row[:half] - row[half:]))
    if even is None:
        return odd + [-value for value in odd]
    return [a + b for a, b in zip(even, odd)] + [a - b for a, b in zip(even, odd)]


def time_kernel(state_ref, out_ref, done_ref, sems):
    row = frequency * kernel_row(NT)
    lines = state_ref.shape[1] // WRITES
    writes = []
    for b in range(WRITES):

        def step(tile, carry):
            rows = pl.ds(pl.multiple_of(b * lines + tile * TILE, TILE), TILE)
            values = [state_ref[n, rows, :] for n in range(NT)]
            for n, value in enumerate(circular_sums(values, row)):
                done_ref[n, rows, :] = value
            return carry

        lax.fori_loop(0, lines // TILE, step, 0)
        rows = slice(b * lines, (b + 1) * lines)
        writes.append(pltpu.make_async_copy(done_ref.at[:, rows], out_ref.at[:, rows], sems.at[b]))
        writes[-1].start()
    for write in writes:
        write.wait()


def time_terms(gathered):
    return pl.pallas_call(
        time_kernel,
        out_shape=jax.ShapeDtypeStruct(gathered.shape, jnp.float32),
        in_specs=[pl.BlockSpec(memory_space=pltpu.VMEM)],
        out_specs=pl.BlockSpec(memory_space=pl.ANY),
        scratch_shapes=[pltpu.VMEM(gathered.shape, jnp.float32), pltpu.SemaphoreType.DMA((WRITES,))],
        compiler_params=pltpu.CompilerParams(vmem_limit_bytes=16 * 2**20),
        cost_estimate=pl.CostEstimate(
            flops=16 * gathered.size, bytes_accessed=8 * gathered.size, transcendentals=0
        ),
    )(gathered)


def primitives(q):
    inverse = 1.0 / q[0]
    speed = [q[1] * inverse, q[2] * inverse, q[3] * inverse]
    pressure = 0.4 * (q[4] - 0.5 * (q[1] * speed[0] + q[2] * speed[1] + q[3] * speed[2]))
    sound = jnp.sqrt(1.4 * pressure * inverse)
    return speed, pressure, sound


def along(speed, sound, normal):
    normal_speed = speed[0] * normal[0] + speed[1] * normal[1] + speed[2] * normal[2]
    area = jnp.sqrt(normal[0] * normal[0] + normal[1] * normal[1] + normal[2] * normal[2])
    return normal_speed, jnp.abs(normal_speed) + sound * area


def flux(v, q, normal_speed, pressure, normal):
    if v in (1, 2, 3):
        return q * normal_speed + pressure * normal[v - 1]
    if v == 4:
        return (q + pressure) * normal_speed
    return q * normal_speed


def spatial_kernel(
    state_ref, halo_ref, metric_ref, metric_halo_ref, volume_ref, out_ref, prim_ref, span_ref
):
    depth, height, width = state_ref.shape[2:]
    n = pl.program_id(0)
    lane = lax.broadcasted_iota(jnp.int32, (height, width), 1)
    first = lane == 0
    last = lane == width - 1
    back = lambda x: pltpu.roll(x, 1, 1)
    ahead = lambda x: pltpu.roll(x, width - 1, 1)
    rows = height + TILE
    down = lambda x: pltpu.roll(x, 1, 0)
    up = lambda x: pltpu.roll(x, rows - 1, 0)

    def prepare(k, carry):
        q = [state_ref[n, v, k] for v in range(6)]
        speed, pressure, sound = primitives(q)
        for v in range(3):
            prim_ref[v, k] = speed[v]
        prim_ref[3, k] = pressure
        prim_ref[4, k] = sound
        normal = [metric_ref[2, c, k] for c in range(3)]
        normal_speed, radius = along(speed, sound, normal)
        span_ref[6, k] = radius
        for v in range(6):
            span_ref[v, k] = flux(v, q[v], normal_speed, pressure, normal)
        return carry

    lax.fori_loop(0, depth, prepare, 0)

    def step(k, carry):
        speed = [prim_ref[v, k] for v in range(3)]
        pressure = prim_ref[3, k]
        sound = prim_ref[4, k]
        halo = [halo_ref[n, v, k] for v in range(6)]
        halo_speed, halo_pressure, halo_sound = primitives(halo)
        join = lambda a, b: jnp.concatenate([a, b], axis=0)
        wrap_normal = [join(metric_ref[0, c, k], metric_halo_ref[c, k]) for c in range(3)]
        wrap_pressure = join(pressure, halo_pressure)
        wrap_speed, wrap_radius = along(
            [join(a, b) for a, b in zip(speed, halo_speed)], join(sound, halo_sound), wrap_normal
        )
        wrap_weight = dissipation * (wrap_radius + down(wrap_radius))
        wall_normal = [metric_ref[1, c, k] for c in range(3)]
        wall_speed, wall_radius = along(speed, sound, wall_normal)
        wall_weight = dissipation * (wall_radius + jnp.where(first, wall_radius, back(wall_radius)))
        wall_end = (2.0 * dissipation) * wall_radius
        volume = volume_ref[k]
        squared = (
            wall_normal[0] * wall_normal[0] + wall_normal[1] * wall_normal[1] + wall_normal[2] * wall_normal[2]
        )
        coefficient = viscosity * (1.0 + state_ref[n, 5, k]) * (squared / volume)
        coefficient = coefficient + back(coefficient)
        k1 = jnp.maximum(k - 1, 0)
        k2 = jnp.maximum(k - 2, 0)
        k3 = jnp.minimum(k + 1, depth - 1)
        k4 = jnp.minimum(k + 2, depth - 1)
        span_low = dissipation * (span_ref[6, k] + span_ref[6, k1])
        span_high = dissipation * (span_ref[6, k] + span_ref[6, k3])

        for v in range(6):
            q = state_ref[n, v, k]
            cells = join(q, halo[v])
            face = flux(v, cells, wrap_speed, wrap_pressure, wrap_normal)
            step_one = cells - down(cells)
            step_two = up(step_one) - step_one
            step_three = step_two - down(step_two)
            face = face + down(face) - wrap_weight * step_three
            total = (up(face) - face)[:height]
            cell = flux(v, q, wall_speed, pressure, wall_normal)
            step_one = jnp.where(first, 0.0, q - back(q))
            step_two = ahead(step_one) - step_one
            step_three = step_two - jnp.where(first, 0.0, back(step_two))
            face = cell + jnp.where(first, cell, back(cell)) - wall_weight * step_three
            if v > 0:
                face = face - coefficient * step_one
            end = 2.0 * cell - wall_end * step_one
            total = total + (jnp.where(last, end, ahead(face)) - face)
            q1 = state_ref[n, v, k1]
            q2 = state_ref[n, v, k2]
            q3 = state_ref[n, v, k3]
            q4 = state_ref[n, v, k4]
            total = total + (span_ref[v, k3] - span_ref[v, k1])
            total = total - span_high * (q4 - q1 - 3.0 * (q3 - q))
            total = total + span_low * (q3 - q2 - 3.0 * (q - q1))
            out_ref[n, v, k] = total
        return carry

    lax.fori_loop(0, depth, step, 0)


def spatial(state, halo, metrics, metric_halo, volume):
    count, variables, depth, height, width = state.shape
    vmem = pl.BlockSpec(memory_space=pltpu.VMEM)
    return pl.pallas_call(
        spatial_kernel,
        grid=(count,),
        out_shape=jax.ShapeDtypeStruct(state.shape, jnp.float32),
        in_specs=[vmem] * 5,
        out_specs=vmem,
        scratch_shapes=[
            pltpu.VMEM((5, depth, height, width), jnp.float32),
            pltpu.VMEM((7, depth, height, width), jnp.float32),
        ],
        compiler_params=pltpu.CompilerParams(vmem_limit_bytes=16 * 2**20),
        cost_estimate=pl.CostEstimate(
            flops=400 * count * depth * height * width,
            bytes_accessed=12 * state.size + 4 * metrics.size,
            transcendentals=0,
        ),
    )(state, halo, metrics, metric_halo, volume)


def combine_kernel(spatial_ref, volume_ref, term_ref, out_ref, done_ref, sems):
    count, variables, depth = spatial_ref.shape[:3]
    parts = term_ref.shape[0] // depth
    run = variables // BLOCKS
    blocks = [(n, slice(b * run, (b + 1) * run)) for n in range(count) for b in range(BLOCKS)]
    writes = [
        pltpu.make_async_copy(done_ref.at[n, r], out_ref.at[n, r], sems.at[b])
        for b, (n, r) in enumerate(blocks)
    ]
    for b, (n, r) in enumerate(blocks):

        def step(k, carry):
            volume = volume_ref[k]
            for v in range(r.start, r.stop):
                term = jnp.concatenate([term_ref[parts * k + p, n, v] for p in range(parts)], axis=0)
                done_ref[n, v, k] = spatial_ref[n, v, k] + volume * term
            return carry

        lax.fori_loop(0, depth, step, 0)
        writes[b].start()
    for write in writes:
        write.wait()


def combined(local, volume, terms):
    vmem = pl.BlockSpec(memory_space=pltpu.VMEM)
    return pl.pallas_call(
        combine_kernel,
        out_shape=jax.ShapeDtypeStruct(local.shape, jnp.float32),
        in_specs=[vmem] * 3,
        out_specs=pl.BlockSpec(memory_space=pl.ANY),
        scratch_shapes=[
            pltpu.VMEM(local.shape, jnp.float32),
            pltpu.SemaphoreType.DMA((local.shape[0] * BLOCKS,)),
        ],
        compiler_params=pltpu.CompilerParams(vmem_limit_bytes=16 * 2**20),
        cost_estimate=pl.CostEstimate(
            flops=2 * local.size, bytes_accessed=12 * local.size, transcendentals=0
        ),
    )(local, volume, terms)


def wrap_halos(state, metrics):
    count = lax.axis_size("wrap")
    onward = [(i, (i + 1) % count) for i in range(count)]
    backward = [((i + 1) % count, i) for i in range(count)]
    inst_count, variables, depth, height, width = state.shape
    pack = lambda cells, face: jnp.concatenate(
        [cells.reshape(-1, width), face.reshape(-1, width)], axis=0
    )
    size = inst_count * variables * depth * 2
    before = lax.ppermute(pack(state[..., -2:, :], metrics[0, :, :, -1:]), "wrap", onward)
    after = lax.ppermute(pack(state[..., :2, :], metrics[0, :, :, :1]), "wrap", backward)
    cells = lambda packed: packed[:size].reshape(inst_count, variables, depth, 2, width)
    face = lambda packed: packed[size:].reshape(3, depth, 1, width)
    halo = jnp.concatenate([cells(after), cells(after), cells(before), cells(before)], axis=-2)
    metric_halo = jnp.concatenate([face(after)] * 4 + [face(before)] * 4, axis=-2)
    return halo, metric_halo


def body(state, metrics, volume):
    inst_count, variables, depth, height, width = state.shape
    owners = lax.axis_size("inst")
    parts = owners // depth
    lines = height // parts
    halo, metric_halo = wrap_halos(state, metrics)
    split = state.reshape(inst_count, variables, depth, parts, lines, width)
    sent = split.transpose(2, 3, 0, 1, 4, 5).reshape(owners, inst_count * variables * lines, width)
    held = lax.all_to_all(sent, "inst", 0, 0, tiled=True)
    terms = time_terms(held.reshape(owners * inst_count, variables * lines, width))
    terms = lax.all_to_all(terms.reshape(sent.shape), "inst", 0, 0, tiled=True)
    terms = terms.reshape(owners, inst_count, variables, lines, width)
    local = spatial(state, halo, metrics, metric_halo, volume)
    return combined(0.5 * local, volume, terms)


def solution(mesh):
    in_specs = (
        P("inst", None, None, "wrap", None),
        P(None, None, None, "wrap", None),
        P(None, "wrap", None),
    )
    out_specs = P("inst", None, None, "wrap", None)
    return jax.shard_map(body, mesh=mesh, in_specs=in_specs, out_specs=out_specs, check_vma=False)
```

```python
import functools
import math

import jax
import jax.numpy as jnp
import numpy as np
from jax import lax
from jax.experimental import pallas as pl
from jax.experimental.pallas import tpu as pltpu
from jax.sharding import PartitionSpec as P

NT = 32
NJ = 128
TILE = 8
FIRST = 62
SECOND = 61
WRITTEN = (8, 4)
WRITES = 4
BLOCKS = 2

dissipation = 0.03125
viscosity = 0.2
frequency = 0.25


def kernel_row(size):
    row = np.zeros(size)
    for k in range(1, size):
        if 2 * k != size:
            row[k] = 0.5 * (-1.0) ** k / math.tan(math.pi * k / size)
    return row


def weighted(pairs):
    total = None
    for weight, value in pairs:
        if abs(weight) > 1e-12:
            term = np.float32(weight) * value
            total = term if total is None else total + term
    return total


def skew_sums(values, row):
    size = len(values)
    half = size // 2
    if size == 2:
        return [-np.float32(row[1]) * values[1], np.float32(row[1]) * values[0]]
    at = lambda k: row[k % size] * (1.0 if (k // size) % 2 == 0 else -1.0)
    even = [values[0]] + [values[m] - values[size - m] for m in range(1, half)]
    odd = [None] + [values[m] + values[size - m] for m in range(1, half)] + [values[half]]
    from_even = [None] + [
        weighted(
            [(at(n), even[0])] + [(0.5 * (at(n - m) + at(n + m)), even[m]) for m in range(1, half)]
        )
        for n in range(1, half + 1)
    ]
    from_odd = [
        weighted(
            [(0.5 * (at(n - m) - at(n + m)), odd[m]) for m in range(1, half)] + [(at(n - half), odd[half])]
        )
        for n in range(half)
    ]
    out = [from_odd[0]] + [from_odd[n] + from_even[n] for n in range(1, half)] + [from_even[half]]
    return out + [from_even[n] - from_odd[n] for n in range(half - 1, 0, -1)]


def circular_sums(values, row):
    size = len(values)
    half = size // 2
    if size == 2:
        return None
    plus = [values[n] + values[n + half] for n in range(half)]
    minus = [values[n] - values[n + half] for n in range(half)]
    even = circular_sums(plus, 0.5 * (row[:half] + row[half:]))
    odd = skew_sums(minus, 0.5 * (row[:half] - row[half:]))
    if even is None:
        return odd + [-value for value in odd]
    return [a + b for a, b in zip(even, odd)] + [a - b for a, b in zip(even, odd)]


def pack_kernel(state_ref, local_ref, sent_ref, sems):
    count, variables, depth, height, width = state_ref.shape
    owners, _, _, lines, _ = sent_ref.shape
    parts = height // lines
    copies = [
        pltpu.make_async_copy(
            state_ref.at[n, :, k, p * lines : (p + 1) * lines],
            sent_ref.at[parts * k + p, n],
            sems.at[n, parts * k + p],
        )
        for k in range(depth)
        for p in range(parts)
        for n in range(count)
    ]
    for copy in copies:
        copy.start()
    for copy in copies:
        copy.wait()


def packed(state, local, owners):
    count, variables, depth, height, width = state.shape
    return pl.pallas_call(
        pack_kernel,
        out_shape=pltpu.VMEM((owners, count, variables, height * depth // owners, width), jnp.float32),
        in_specs=[pl.BlockSpec(memory_space=pl.ANY)] * 2,
        out_specs=pl.BlockSpec(memory_space=pltpu.VMEM),
        scratch_shapes=[pltpu.SemaphoreType.DMA((count, owners))],
        compiler_params=pltpu.CompilerParams(vmem_limit_bytes=61 * 2**20),
        cost_estimate=pl.CostEstimate(flops=0, bytes_accessed=8 * state.size, transcendentals=0),
    )(state, local)


def time_kernel(state_ref, out_ref, done_ref, sems):
    row = frequency * kernel_row(NT)
    lines = state_ref.shape[1] // WRITES
    writes = []
    for b in range(WRITES):

        def step(tile, carry):
            rows = pl.ds(pl.multiple_of(b * lines + tile * TILE, TILE), TILE)
            values = [state_ref[n, rows, :] for n in range(NT)]
            for n, value in enumerate(circular_sums(values, row)):
                done_ref[n, rows, :] = value
            return carry

        lax.fori_loop(0, lines // TILE, step, 0)
        rows = slice(b * lines, (b + 1) * lines)
        writes.append(pltpu.make_async_copy(done_ref.at[:, rows], out_ref.at[:, rows], sems.at[b]))
        writes[-1].start()
    for write in writes:
        write.wait()


def time_terms(gathered):
    return pl.pallas_call(
        time_kernel,
        out_shape=jax.ShapeDtypeStruct(gathered.shape, jnp.float32),
        in_specs=[pl.BlockSpec(memory_space=pltpu.VMEM)],
        out_specs=pl.BlockSpec(memory_space=pl.ANY),
        scratch_shapes=[pltpu.VMEM(gathered.shape, jnp.float32), pltpu.SemaphoreType.DMA((WRITES,))],
        compiler_params=pltpu.CompilerParams(vmem_limit_bytes=16 * 2**20),
        cost_estimate=pl.CostEstimate(
            flops=16 * gathered.size, bytes_accessed=8 * gathered.size, transcendentals=0
        ),
    )(gathered)


def primitives(q):
    inverse = 1.0 / q[0]
    speed = [q[1] * inverse, q[2] * inverse, q[3] * inverse]
    pressure = 0.4 * (q[4] - 0.5 * (q[1] * speed[0] + q[2] * speed[1] + q[3] * speed[2]))
    sound = jnp.sqrt(1.4 * pressure * inverse)
    return speed, pressure, sound


def along(speed, sound, normal):
    normal_speed = speed[0] * normal[0] + speed[1] * normal[1] + speed[2] * normal[2]
    area = jnp.sqrt(normal[0] * normal[0] + normal[1] * normal[1] + normal[2] * normal[2])
    return normal_speed, jnp.abs(normal_speed) + sound * area


def flux(v, q, normal_speed, pressure, normal):
    if v in (1, 2, 3):
        return q * normal_speed + pressure * normal[v - 1]
    if v == 4:
        return (q + pressure) * normal_speed
    return q * normal_speed


def cross_instance(n, writes, state_ref, metric_ref, volume_ref, out_ref, span_ref, out_hbm, sem):
    depth, height, width = state_ref.shape[2:]
    lane = lax.broadcasted_iota(jnp.int32, (height, width), 1)
    first = lane == 0
    last = lane == width - 1
    back = lambda x: pltpu.roll(x, 1, 1)
    ahead = lambda x: pltpu.roll(x, width - 1, 1)

    def prepare(k, carry):
        q = [state_ref[n, v, k] for v in range(6)]
        speed, pressure, sound = primitives(q)
        for v in range(3):
            span_ref[7 + v, k] = speed[v]
        span_ref[10, k] = pressure
        span_ref[11, k] = sound
        normal = [metric_ref[2, c, k] for c in range(3)]
        normal_speed, radius = along(speed, sound, normal)
        span_ref[6, k] = radius
        for v in range(6):
            span_ref[v, k] = flux(v, q[v], normal_speed, pressure, normal)
        return carry

    lax.fori_loop(0, depth, prepare, 0)

    def step(k, carry):
        speed = [span_ref[7 + v, k] for v in range(3)]
        pressure = span_ref[10, k]
        sound = span_ref[11, k]
        wall_normal = [metric_ref[1, c, k] for c in range(3)]
        wall_speed, wall_radius = along(speed, sound, wall_normal)
        wall_weight = dissipation * (wall_radius + jnp.where(first, wall_radius, back(wall_radius)))
        wall_end = (2.0 * dissipation) * wall_radius
        squared = (
            wall_normal[0] * wall_normal[0] + wall_normal[1] * wall_normal[1] + wall_normal[2] * wall_normal[2]
        )
        coefficient = viscosity * (1.0 + state_ref[n, 5, k]) * (squared / volume_ref[k])
        coefficient = coefficient + back(coefficient)
        k1 = jnp.maximum(k - 1, 0)
        k2 = jnp.maximum(k - 2, 0)
        k3 = jnp.minimum(k + 1, depth - 1)
        k4 = jnp.minimum(k + 2, depth - 1)
        span_low = dissipation * (span_ref[6, k] + span_ref[6, k1])
        span_high = dissipation * (span_ref[6, k] + span_ref[6, k3])
        for v in range(6):
            q = state_ref[n, v, k]
            cell = flux(v, q, wall_speed, pressure, wall_normal)
            step_one = jnp.where(first, 0.0, q - back(q))
            step_two = ahead(step_one) - step_one
            step_three = step_two - jnp.where(first, 0.0, back(step_two))
            face = cell + jnp.where(first, cell, back(cell)) - wall_weight * step_three
            if v > 0:
                face = face - coefficient * step_one
            end = 2.0 * cell - wall_end * step_one
            total = jnp.where(last, end, ahead(face)) - face
            q1 = state_ref[n, v, k1]
            q2 = state_ref[n, v, k2]
            q3 = state_ref[n, v, k3]
            q4 = state_ref[n, v, k4]
            total = total + (span_ref[v, k3] - span_ref[v, k1])
            total = total - span_high * (q4 - q1 - 3.0 * (q3 - q))
            total = total + span_low * (q3 - q2 - 3.0 * (q - q1))
            out_ref[v, k] = total
        return carry

    run = depth // writes

    def write(r, carry):
        lax.fori_loop(r * run, (r + 1) * run, step, 0)
        done = pltpu.make_async_copy(
            out_ref.at[:, pl.ds(r * run, run)], out_hbm.at[n, :, pl.ds(r * run, run)], sem
        )
        done.start()
        done.wait()
        return carry

    lax.fori_loop(0, writes, write, 0)


def cross_kernel(
    turn, state_hbm, metric_hbm, volume_hbm, out_hbm,
    state_ref, metric_ref, volume_ref, out_ref, span_ref, in_sems, out_sem,
):
    count = state_ref.shape[0]

    @pl.when(lax.axis_index("wrap") % 2 == turn)
    def _():
        fetches = [
            pltpu.make_async_copy(metric_hbm, metric_ref, in_sems.at[0]),
            pltpu.make_async_copy(volume_hbm, volume_ref, in_sems.at[1]),
            pltpu.make_async_copy(state_hbm, state_ref, in_sems.at[2]),
        ]
        for fetch in fetches:
            fetch.start()
        for fetch in fetches:
            fetch.wait()

        for n in range(count):
            cross_instance(
                n, WRITTEN[n % len(WRITTEN)], state_ref, metric_ref, volume_ref, out_ref, span_ref, out_hbm, out_sem
            )


def cross(turn, limit, state, metrics, volume):
    count, variables, depth, height, width = state.shape
    anywhere = pl.BlockSpec(memory_space=pl.ANY)
    slabs = lambda size: pltpu.VMEM((size, depth, height, width), jnp.float32)
    return pl.pallas_call(
        functools.partial(cross_kernel, turn),
        out_shape=jax.ShapeDtypeStruct(state.shape, jnp.float32),
        in_specs=[anywhere] * 3,
        out_specs=anywhere,
        scratch_shapes=[
            pltpu.VMEM(state.shape, jnp.float32),
            pltpu.VMEM(metrics.shape, jnp.float32),
            pltpu.VMEM(volume.shape, jnp.float32),
            slabs(variables),
            slabs(12),
            pltpu.SemaphoreType.DMA((3,)),
            pltpu.SemaphoreType.DMA(()),
        ],
        compiler_params=pltpu.CompilerParams(vmem_limit_bytes=limit * 2**20),
        cost_estimate=pl.CostEstimate(
            flops=300 * count * depth * height * width,
            bytes_accessed=12 * state.size + 4 * metrics.size,
            transcendentals=0,
        ),
    )(state, metrics, volume)


def wrap_kernel(
    state_ref, halo_ref, metric_ref, metric_halo_ref, early_hbm, late_hbm, out_ref, cross_ref, sem
):
    depth, height, width = state_ref.shape[2:]
    n = pl.program_id(0)
    rows = height + TILE
    down = lambda x: pltpu.roll(x, 1, 0)
    up = lambda x: pltpu.roll(x, rows - 1, 0)
    join = lambda a, b: jnp.concatenate([a, b], axis=0)
    for turn, ref in enumerate([late_hbm, early_hbm]):

        @pl.when(lax.axis_index("wrap") % 2 == turn)
        def _():
            fetch = pltpu.make_async_copy(ref.at[n], cross_ref, sem)
            fetch.start()
            fetch.wait()

    def step(k, carry):
        q = [join(state_ref[n, v, k], halo_ref[n, v, k]) for v in range(6)]
        speed, pressure, sound = primitives(q)
        normal = [join(metric_ref[0, c, k], metric_halo_ref[c, k]) for c in range(3)]
        normal_speed, radius = along(speed, sound, normal)
        weight = dissipation * (radius + down(radius))
        for v in range(6):
            face = flux(v, q[v], normal_speed, pressure, normal)
            step_one = q[v] - down(q[v])
            step_two = up(step_one) - step_one
            step_three = step_two - down(step_two)
            face = face + down(face) - weight * step_three
            out_ref[n, v, k] = cross_ref[v, k] + (up(face) - face)[:height]
        return carry

    lax.fori_loop(0, depth, step, 0)


def with_wrap(state, halo, metrics, metric_halo, early, late):
    vmem = pl.BlockSpec(memory_space=pltpu.VMEM)
    return pl.pallas_call(
        wrap_kernel,
        grid=(state.shape[0],),
        out_shape=jax.ShapeDtypeStruct(state.shape, jnp.float32),
        in_specs=[vmem] * 4 + [pl.BlockSpec(memory_space=pl.ANY)] * 2,
        out_specs=vmem,
        scratch_shapes=[pltpu.VMEM(state.shape[1:], jnp.float32), pltpu.SemaphoreType.DMA(())],
        compiler_params=pltpu.CompilerParams(vmem_limit_bytes=16 * 2**20),
        cost_estimate=pl.CostEstimate(
            flops=30 * state.size, bytes_accessed=12 * state.size + 4 * metrics.size, transcendentals=0
        ),
    )(state, halo, metrics, metric_halo, early, late)


def combine_kernel(spatial_ref, volume_ref, term_hbm, out_hbm, term_ref, done_ref, in_sems, out_sems):
    count, variables, depth = spatial_ref.shape[:3]
    parts = term_ref.shape[0] // depth
    run = variables // BLOCKS
    blocks = [(n, slice(b * run, (b + 1) * run)) for n in range(count) for b in range(BLOCKS)]
    fetches = [
        pltpu.make_async_copy(term_hbm.at[:, n, r], term_ref.at[:, n, r], in_sems.at[b])
        for b, (n, r) in enumerate(blocks)
    ]
    writes = [
        pltpu.make_async_copy(done_ref.at[n, r], out_hbm.at[n, r], out_sems.at[b])
        for b, (n, r) in enumerate(blocks)
    ]
    for fetch in fetches:
        fetch.start()
    for b, (n, r) in enumerate(blocks):
        fetches[b].wait()

        def step(k, carry):
            volume = volume_ref[k]
            for v in range(r.start, r.stop):
                term = jnp.concatenate([term_ref[parts * k + p, n, v] for p in range(parts)], axis=0)
                done_ref[n, v, k] = spatial_ref[n, v, k] + volume * term
            return carry

        lax.fori_loop(0, depth, step, 0)
        writes[b].start()
    for write in writes:
        write.wait()


def combined(local, volume, terms):
    vmem = pl.BlockSpec(memory_space=pltpu.VMEM)
    anywhere = pl.BlockSpec(memory_space=pl.ANY)
    count = local.shape[0] * BLOCKS
    return pl.pallas_call(
        combine_kernel,
        out_shape=jax.ShapeDtypeStruct(local.shape, jnp.float32),
        in_specs=[vmem] * 2 + [anywhere],
        out_specs=anywhere,
        scratch_shapes=[
            pltpu.VMEM(terms.shape, jnp.float32),
            pltpu.VMEM(local.shape, jnp.float32),
            pltpu.SemaphoreType.DMA((count,)),
            pltpu.SemaphoreType.DMA((count,)),
        ],
        compiler_params=pltpu.CompilerParams(vmem_limit_bytes=16 * 2**20),
        cost_estimate=pl.CostEstimate(
            flops=2 * local.size, bytes_accessed=12 * local.size, transcendentals=0
        ),
    )(local, volume, terms)


def wrap_halos(state, metrics):
    count = lax.axis_size("wrap")
    onward = [(i, (i + 1) % count) for i in range(count)]
    backward = [((i + 1) % count, i) for i in range(count)]
    inst_count, variables, depth, height, width = state.shape
    pack = lambda cells, face: jnp.concatenate(
        [cells.reshape(-1, width), face.reshape(-1, width)], axis=0
    )
    size = inst_count * variables * depth * 2
    before = lax.ppermute(pack(state[..., -2:, :], metrics[0, :, :, -1:]), "wrap", onward)
    after = lax.ppermute(pack(state[..., :2, :], metrics[0, :, :, :1]), "wrap", backward)
    cells = lambda packed: packed[:size].reshape(inst_count, variables, depth, 2, width)
    face = lambda packed: packed[size:].reshape(3, depth, 1, width)
    halo = jnp.concatenate([cells(after), cells(after), cells(before), cells(before)], axis=-2)
    metric_halo = jnp.concatenate([face(after)] * 4 + [face(before)] * 4, axis=-2)
    return halo, metric_halo


def body(state, metrics, volume):
    inst_count, variables, depth, height, width = state.shape
    owners = lax.axis_size("inst")
    parts = owners // depth
    lines = height // parts
    early = cross(1, FIRST, state, metrics, volume)
    sent = packed(state, early, owners).reshape(owners, inst_count * variables * lines, width)
    held = lax.all_to_all(sent, "inst", 0, 0, tiled=True)
    terms = time_terms(held.reshape(owners * inst_count, variables * lines, width))
    terms = lax.all_to_all(terms.reshape(sent.shape), "inst", 0, 0, tiled=True)
    terms = terms.reshape(owners, inst_count, variables, lines, width)
    late = cross(0, SECOND, state, metrics, volume)
    after, late = lax.optimization_barrier((state, late))
    halo, metric_halo = wrap_halos(after, metrics)
    local = with_wrap(state, halo, metrics, metric_halo, early, late)
    return combined(0.5 * local, volume, terms)


def solution(mesh):
    in_specs = (
        P("inst", None, None, "wrap", None),
        P(None, None, None, "wrap", None),
        P(None, "wrap", None),
    )
    out_specs = P("inst", None, None, "wrap", None)
    return jax.shard_map(body, mesh=mesh, in_specs=in_specs, out_specs=out_specs, check_vma=False)
```

```python
import functools
import math

import jax
import jax.numpy as jnp
import numpy as np
from jax import lax
from jax.experimental import pallas as pl
from jax.experimental.pallas import tpu as pltpu
from jax.sharding import PartitionSpec as P

NT = 32
NJ = 128
TILE = 8
FIRST = 62
SECOND = 61
EARLY = (4, 4)
LATE = (1, 1)
WRITES = 4
BLOCKS = 2

dissipation = 0.03125
viscosity = 0.2
frequency = 0.25


def kernel_row(size):
    row = np.zeros(size)
    for k in range(1, size):
        if 2 * k != size:
            row[k] = 0.5 * (-1.0) ** k / math.tan(math.pi * k / size)
    return row


def weighted(pairs):
    total = None
    for weight, value in pairs:
        if abs(weight) > 1e-12:
            term = np.float32(weight) * value
            total = term if total is None else total + term
    return total


def skew_sums(values, row):
    size = len(values)
    half = size // 2
    if size == 2:
        return [-np.float32(row[1]) * values[1], np.float32(row[1]) * values[0]]
    at = lambda k: row[k % size] * (1.0 if (k // size) % 2 == 0 else -1.0)
    even = [values[0]] + [values[m] - values[size - m] for m in range(1, half)]
    odd = [None] + [values[m] + values[size - m] for m in range(1, half)] + [values[half]]
    from_even = [None] + [
        weighted(
            [(at(n), even[0])] + [(0.5 * (at(n - m) + at(n + m)), even[m]) for m in range(1, half)]
        )
        for n in range(1, half + 1)
    ]
    from_odd = [
        weighted(
            [(0.5 * (at(n - m) - at(n + m)), odd[m]) for m in range(1, half)] + [(at(n - half), odd[half])]
        )
        for n in range(half)
    ]
    out = [from_odd[0]] + [from_odd[n] + from_even[n] for n in range(1, half)] + [from_even[half]]
    return out + [from_even[n] - from_odd[n] for n in range(half - 1, 0, -1)]


def circular_sums(values, row):
    size = len(values)
    half = size // 2
    if size == 2:
        return None
    plus = [values[n] + values[n + half] for n in range(half)]
    minus = [values[n] - values[n + half] for n in range(half)]
    even = circular_sums(plus, 0.5 * (row[:half] + row[half:]))
    odd = skew_sums(minus, 0.5 * (row[:half] - row[half:]))
    if even is None:
        return odd + [-value for value in odd]
    return [a + b for a, b in zip(even, odd)] + [a - b for a, b in zip(even, odd)]


def pack_kernel(state_ref, local_ref, sent_ref, sems):
    count, variables, depth, height, width = state_ref.shape
    owners, _, _, lines, _ = sent_ref.shape
    parts = height // lines
    copies = [
        pltpu.make_async_copy(
            state_ref.at[n, :, k, p * lines : (p + 1) * lines],
            sent_ref.at[parts * k + p, n],
            sems.at[n, parts * k + p],
        )
        for k in range(depth)
        for p in range(parts)
        for n in range(count)
    ]
    for copy in copies:
        copy.start()
    for copy in copies:
        copy.wait()


def packed(state, local, owners):
    count, variables, depth, height, width = state.shape
    return pl.pallas_call(
        pack_kernel,
        out_shape=pltpu.VMEM((owners, count, variables, height * depth // owners, width), jnp.float32),
        in_specs=[pl.BlockSpec(memory_space=pl.ANY)] * 2,
        out_specs=pl.BlockSpec(memory_space=pltpu.VMEM),
        scratch_shapes=[pltpu.SemaphoreType.DMA((count, owners))],
        compiler_params=pltpu.CompilerParams(vmem_limit_bytes=61 * 2**20),
        cost_estimate=pl.CostEstimate(flops=0, bytes_accessed=8 * state.size, transcendentals=0),
    )(state, local)


def time_kernel(state_ref, out_ref, done_ref, sems):
    row = frequency * kernel_row(NT)
    lines = state_ref.shape[1] // WRITES
    writes = []
    for b in range(WRITES):

        def step(tile, carry):
            rows = pl.ds(pl.multiple_of(b * lines + tile * TILE, TILE), TILE)
            values = [state_ref[n, rows, :] for n in range(NT)]
            for n, value in enumerate(circular_sums(values, row)):
                done_ref[n, rows, :] = value
            return carry

        lax.fori_loop(0, lines // TILE, step, 0)
        rows = slice(b * lines, (b + 1) * lines)
        writes.append(pltpu.make_async_copy(done_ref.at[:, rows], out_ref.at[:, rows], sems.at[b]))
        writes[-1].start()
    for write in writes:
        write.wait()


def time_terms(gathered):
    return pl.pallas_call(
        time_kernel,
        out_shape=jax.ShapeDtypeStruct(gathered.shape, jnp.float32),
        in_specs=[pl.BlockSpec(memory_space=pltpu.VMEM)],
        out_specs=pl.BlockSpec(memory_space=pl.ANY),
        scratch_shapes=[pltpu.VMEM(gathered.shape, jnp.float32), pltpu.SemaphoreType.DMA((WRITES,))],
        compiler_params=pltpu.CompilerParams(vmem_limit_bytes=61 * 2**20),
        cost_estimate=pl.CostEstimate(
            flops=16 * gathered.size, bytes_accessed=8 * gathered.size, transcendentals=0
        ),
    )(gathered)


def primitives(q):
    inverse = 1.0 / q[0]
    speed = [q[1] * inverse, q[2] * inverse, q[3] * inverse]
    pressure = 0.4 * (q[4] - 0.5 * (q[1] * speed[0] + q[2] * speed[1] + q[3] * speed[2]))
    sound = jnp.sqrt(1.4 * pressure * inverse)
    return speed, pressure, sound


def along(speed, sound, normal):
    normal_speed = speed[0] * normal[0] + speed[1] * normal[1] + speed[2] * normal[2]
    area = jnp.sqrt(normal[0] * normal[0] + normal[1] * normal[1] + normal[2] * normal[2])
    return normal_speed, jnp.abs(normal_speed) + sound * area


def flux(v, q, normal_speed, pressure, normal):
    if v in (1, 2, 3):
        return q * normal_speed + pressure * normal[v - 1]
    if v == 4:
        return (q + pressure) * normal_speed
    return q * normal_speed


def cross_instance(n, writes, state_ref, metric_ref, volume_ref, out_ref, span_ref, out_hbm, sem):
    depth, height, width = state_ref.shape[2:]
    lane = lax.broadcasted_iota(jnp.int32, (height, width), 1)
    first = lane == 0
    last = lane == width - 1
    back = lambda x: pltpu.roll(x, 1, 1)
    ahead = lambda x: pltpu.roll(x, width - 1, 1)

    def prepare(k, carry):
        q = [state_ref[n, v, k] for v in range(6)]
        speed, pressure, sound = primitives(q)
        for v in range(3):
            span_ref[7 + v, k] = speed[v]
        span_ref[10, k] = pressure
        span_ref[11, k] = sound
        normal = [metric_ref[2, c, k] for c in range(3)]
        normal_speed, radius = along(speed, sound, normal)
        span_ref[6, k] = radius
        for v in range(6):
            span_ref[v, k] = flux(v, q[v], normal_speed, pressure, normal)
        return carry

    lax.fori_loop(0, depth, prepare, 0)

    def step(k, carry):
        speed = [span_ref[7 + v, k] for v in range(3)]
        pressure = span_ref[10, k]
        sound = span_ref[11, k]
        wall_normal = [metric_ref[1, c, k] for c in range(3)]
        wall_speed, wall_radius = along(speed, sound, wall_normal)
        wall_weight = dissipation * (wall_radius + jnp.where(first, wall_radius, back(wall_radius)))
        wall_end = (2.0 * dissipation) * wall_radius
        squared = (
            wall_normal[0] * wall_normal[0] + wall_normal[1] * wall_normal[1] + wall_normal[2] * wall_normal[2]
        )
        coefficient = viscosity * (1.0 + state_ref[n, 5, k]) * (squared / volume_ref[k])
        coefficient = coefficient + back(coefficient)
        k1 = jnp.maximum(k - 1, 0)
        k2 = jnp.maximum(k - 2, 0)
        k3 = jnp.minimum(k + 1, depth - 1)
        k4 = jnp.minimum(k + 2, depth - 1)
        span_low = dissipation * (span_ref[6, k] + span_ref[6, k1])
        span_high = dissipation * (span_ref[6, k] + span_ref[6, k3])
        for v in range(6):
            q = state_ref[n, v, k]
            cell = flux(v, q, wall_speed, pressure, wall_normal)
            step_one = jnp.where(first, 0.0, q - back(q))
            step_two = ahead(step_one) - step_one
            step_three = step_two - jnp.where(first, 0.0, back(step_two))
            face = cell + jnp.where(first, cell, back(cell)) - wall_weight * step_three
            if v > 0:
                face = face - coefficient * step_one
            end = 2.0 * cell - wall_end * step_one
            total = jnp.where(last, end, ahead(face)) - face
            q1 = state_ref[n, v, k1]
            q2 = state_ref[n, v, k2]
            q3 = state_ref[n, v, k3]
            q4 = state_ref[n, v, k4]
            total = total + (span_ref[v, k3] - span_ref[v, k1])
            total = total - span_high * (q4 - q1 - 3.0 * (q3 - q))
            total = total + span_low * (q3 - q2 - 3.0 * (q - q1))
            out_ref[v, k] = total
        return carry

    run = depth // writes

    def write(r, carry):
        lax.fori_loop(r * run, (r + 1) * run, step, 0)
        done = pltpu.make_async_copy(
            out_ref.at[:, pl.ds(r * run, run)], out_hbm.at[n, :, pl.ds(r * run, run)], sem
        )
        done.start()
        done.wait()
        return carry

    lax.fori_loop(0, writes, write, 0)


def cross_kernel(
    turn, writes, state_hbm, metric_hbm, volume_hbm, out_hbm,
    state_ref, metric_ref, volume_ref, out_ref, span_ref, in_sems, out_sem,
):
    count = state_ref.shape[0]

    @pl.when(lax.axis_index("wrap") % 2 == turn)
    def _():
        fetches = [
            pltpu.make_async_copy(metric_hbm, metric_ref, in_sems.at[0]),
            pltpu.make_async_copy(volume_hbm, volume_ref, in_sems.at[1]),
            pltpu.make_async_copy(state_hbm, state_ref, in_sems.at[2]),
        ]
        for fetch in fetches:
            fetch.start()
        for fetch in fetches:
            fetch.wait()

        for n in range(count):
            cross_instance(
                n, writes[n % len(writes)], state_ref, metric_ref, volume_ref, out_ref, span_ref, out_hbm, out_sem
            )


def cross(turn, writes, limit, state, metrics, volume):
    count, variables, depth, height, width = state.shape
    anywhere = pl.BlockSpec(memory_space=pl.ANY)
    slabs = lambda size: pltpu.VMEM((size, depth, height, width), jnp.float32)
    return pl.pallas_call(
        functools.partial(cross_kernel, turn, writes),
        out_shape=jax.ShapeDtypeStruct(state.shape, jnp.float32),
        in_specs=[anywhere] * 3,
        out_specs=anywhere,
        scratch_shapes=[
            pltpu.VMEM(state.shape, jnp.float32),
            pltpu.VMEM(metrics.shape, jnp.float32),
            pltpu.VMEM(volume.shape, jnp.float32),
            slabs(variables),
            slabs(12),
            pltpu.SemaphoreType.DMA((3,)),
            pltpu.SemaphoreType.DMA(()),
        ],
        compiler_params=pltpu.CompilerParams(vmem_limit_bytes=limit * 2**20),
        cost_estimate=pl.CostEstimate(
            flops=300 * count * depth * height * width,
            bytes_accessed=12 * state.size + 4 * metrics.size,
            transcendentals=0,
        ),
    )(state, metrics, volume)


def wrap_kernel(
    state_ref, halo_ref, metric_ref, metric_halo_ref, early_hbm, late_hbm, out_ref, cross_ref, sem
):
    depth, height, width = state_ref.shape[2:]
    n = pl.program_id(0)
    rows = height + TILE
    down = lambda x: pltpu.roll(x, 1, 0)
    up = lambda x: pltpu.roll(x, rows - 1, 0)
    join = lambda a, b: jnp.concatenate([a, b], axis=0)
    for turn, ref in enumerate([early_hbm, late_hbm]):

        @pl.when(lax.axis_index("wrap") % 2 == turn)
        def _():
            fetch = pltpu.make_async_copy(ref.at[n], cross_ref, sem)
            fetch.start()
            fetch.wait()

    def step(k, carry):
        q = [join(state_ref[n, v, k], halo_ref[n, v, k]) for v in range(6)]
        speed, pressure, sound = primitives(q)
        normal = [join(metric_ref[0, c, k], metric_halo_ref[c, k]) for c in range(3)]
        normal_speed, radius = along(speed, sound, normal)
        weight = dissipation * (radius + down(radius))
        for v in range(6):
            face = flux(v, q[v], normal_speed, pressure, normal)
            step_one = q[v] - down(q[v])
            step_two = up(step_one) - step_one
            step_three = step_two - down(step_two)
            face = face + down(face) - weight * step_three
            out_ref[n, v, k] = cross_ref[v, k] + (up(face) - face)[:height]
        return carry

    lax.fori_loop(0, depth, step, 0)


def with_wrap(state, halo, metrics, metric_halo, early, late):
    vmem = pl.BlockSpec(memory_space=pltpu.VMEM)
    return pl.pallas_call(
        wrap_kernel,
        grid=(state.shape[0],),
        out_shape=jax.ShapeDtypeStruct(state.shape, jnp.float32),
        in_specs=[vmem] * 4 + [pl.BlockSpec(memory_space=pl.ANY)] * 2,
        out_specs=vmem,
        scratch_shapes=[pltpu.VMEM(state.shape[1:], jnp.float32), pltpu.SemaphoreType.DMA(())],
        compiler_params=pltpu.CompilerParams(vmem_limit_bytes=16 * 2**20),
        cost_estimate=pl.CostEstimate(
            flops=30 * state.size, bytes_accessed=12 * state.size + 4 * metrics.size, transcendentals=0
        ),
    )(state, halo, metrics, metric_halo, early, late)


def combine_kernel(spatial_ref, volume_ref, term_hbm, out_hbm, term_ref, done_ref, in_sems, out_sems):
    count, variables, depth = spatial_ref.shape[:3]
    parts = term_ref.shape[0] // depth
    run = variables // BLOCKS
    blocks = [(n, slice(b * run, (b + 1) * run)) for n in range(count) for b in range(BLOCKS)]
    fetches = [
        pltpu.make_async_copy(term_hbm.at[:, n, r], term_ref.at[:, n, r], in_sems.at[b])
        for b, (n, r) in enumerate(blocks)
    ]
    writes = [
        pltpu.make_async_copy(done_ref.at[n, r], out_hbm.at[n, r], out_sems.at[b])
        for b, (n, r) in enumerate(blocks)
    ]
    for fetch in fetches:
        fetch.start()
    for b, (n, r) in enumerate(blocks):
        fetches[b].wait()

        def step(k, carry):
            volume = volume_ref[k]
            for v in range(r.start, r.stop):
                term = jnp.concatenate([term_ref[parts * k + p, n, v] for p in range(parts)], axis=0)
                done_ref[n, v, k] = spatial_ref[n, v, k] + volume * term
            return carry

        lax.fori_loop(0, depth, step, 0)
        writes[b].start()
    for write in writes:
        write.wait()


def combined(local, volume, terms):
    vmem = pl.BlockSpec(memory_space=pltpu.VMEM)
    anywhere = pl.BlockSpec(memory_space=pl.ANY)
    count = local.shape[0] * BLOCKS
    return pl.pallas_call(
        combine_kernel,
        out_shape=jax.ShapeDtypeStruct(local.shape, jnp.float32),
        in_specs=[vmem] * 2 + [anywhere],
        out_specs=anywhere,
        scratch_shapes=[
            pltpu.VMEM(terms.shape, jnp.float32),
            pltpu.VMEM(local.shape, jnp.float32),
            pltpu.SemaphoreType.DMA((count,)),
            pltpu.SemaphoreType.DMA((count,)),
        ],
        compiler_params=pltpu.CompilerParams(vmem_limit_bytes=16 * 2**20),
        cost_estimate=pl.CostEstimate(
            flops=2 * local.size, bytes_accessed=12 * local.size, transcendentals=0
        ),
    )(local, volume, terms)


def wrap_halos(state, metrics):
    count = lax.axis_size("wrap")
    onward = [(i, (i + 1) % count) for i in range(count)]
    backward = [((i + 1) % count, i) for i in range(count)]
    inst_count, variables, depth, height, width = state.shape
    pack = lambda cells, face: jnp.concatenate(
        [cells.reshape(-1, width), face.reshape(-1, width)], axis=0
    )
    size = inst_count * variables * depth * 2
    before = lax.ppermute(pack(state[..., -2:, :], metrics[0, :, :, -1:]), "wrap", onward)
    after = lax.ppermute(pack(state[..., :2, :], metrics[0, :, :, :1]), "wrap", backward)
    cells = lambda packed: packed[:size].reshape(inst_count, variables, depth, 2, width)
    face = lambda packed: packed[size:].reshape(3, depth, 1, width)
    halo = jnp.concatenate([cells(after), cells(after), cells(before), cells(before)], axis=-2)
    metric_halo = jnp.concatenate([face(after)] * 4 + [face(before)] * 4, axis=-2)
    return halo, metric_halo


def body(state, metrics, volume):
    inst_count, variables, depth, height, width = state.shape
    owners = lax.axis_size("inst")
    parts = owners // depth
    lines = height // parts
    early = cross(0, EARLY, FIRST, state, metrics, volume)
    sent = packed(state, early, owners).reshape(owners, inst_count * variables * lines, width)
    held = lax.all_to_all(sent, "inst", 0, 0, tiled=True)
    terms = time_terms(held.reshape(owners * inst_count, variables * lines, width))
    terms = lax.all_to_all(terms.reshape(sent.shape), "inst", 0, 0, tiled=True)
    terms = terms.reshape(owners, inst_count, variables, lines, width)
    late = cross(1, LATE, SECOND, state, metrics, volume)
    after, late = lax.optimization_barrier((state, late))
    halo, metric_halo = wrap_halos(after, metrics)
    local = with_wrap(state, halo, metrics, metric_halo, early, late)
    return combined(0.5 * local, volume, terms)


def solution(mesh):
    in_specs = (
        P("inst", None, None, "wrap", None),
        P(None, None, None, "wrap", None),
        P(None, "wrap", None),
    )
    out_specs = P("inst", None, None, "wrap", None)
    return jax.shard_map(body, mesh=mesh, in_specs=in_specs, out_specs=out_specs, check_vma=False)
```

```python
import functools
import math

import jax
import jax.numpy as jnp
import numpy as np
from jax import lax
from jax.experimental import pallas as pl
from jax.experimental.pallas import tpu as pltpu
from jax.sharding import PartitionSpec as P

NT = 32
NJ = 128
TILE = 8
FIRST = 62
SECOND = 61
EARLY = (4, 2)
LATE = (1, 1)
WRITES = 6
BLOCKS = 2

dissipation = 0.03125
viscosity = 0.2
frequency = 0.25


def kernel_row(size):
    row = np.zeros(size)
    for k in range(1, size):
        if 2 * k != size:
            row[k] = 0.5 * (-1.0) ** k / math.tan(math.pi * k / size)
    return row


def weighted(pairs):
    total = None
    for weight, value in pairs:
        if abs(weight) > 1e-12:
            term = np.float32(weight) * value
            total = term if total is None else total + term
    return total


def skew_sums(values, row):
    size = len(values)
    half = size // 2
    if size == 2:
        return [-np.float32(row[1]) * values[1], np.float32(row[1]) * values[0]]
    at = lambda k: row[k % size] * (1.0 if (k // size) % 2 == 0 else -1.0)
    even = [values[0]] + [values[m] - values[size - m] for m in range(1, half)]
    odd = [None] + [values[m] + values[size - m] for m in range(1, half)] + [values[half]]
    from_even = [None] + [
        weighted(
            [(at(n), even[0])] + [(0.5 * (at(n - m) + at(n + m)), even[m]) for m in range(1, half)]
        )
        for n in range(1, half + 1)
    ]
    from_odd = [
        weighted(
            [(0.5 * (at(n - m) - at(n + m)), odd[m]) for m in range(1, half)] + [(at(n - half), odd[half])]
        )
        for n in range(half)
    ]
    out = [from_odd[0]] + [from_odd[n] + from_even[n] for n in range(1, half)] + [from_even[half]]
    return out + [from_even[n] - from_odd[n] for n in range(half - 1, 0, -1)]


def circular_sums(values, row):
    size = len(values)
    half = size // 2
    if size == 2:
        return None
    plus = [values[n] + values[n + half] for n in range(half)]
    minus = [values[n] - values[n + half] for n in range(half)]
    even = circular_sums(plus, 0.5 * (row[:half] + row[half:]))
    odd = skew_sums(minus, 0.5 * (row[:half] - row[half:]))
    if even is None:
        return odd + [-value for value in odd]
    return [a + b for a, b in zip(even, odd)] + [a - b for a, b in zip(even, odd)]


def pack_kernel(state_ref, local_ref, sent_ref, sems):
    count, variables, depth, height, width = state_ref.shape
    owners, _, _, lines, _ = sent_ref.shape
    parts = height // lines
    copies = [
        pltpu.make_async_copy(
            state_ref.at[n, :, k, p * lines : (p + 1) * lines],
            sent_ref.at[parts * k + p, n],
            sems.at[n, parts * k + p],
        )
        for k in range(depth)
        for p in range(parts)
        for n in range(count)
    ]
    for copy in copies:
        copy.start()
    for copy in copies:
        copy.wait()


def packed(state, local, owners):
    count, variables, depth, height, width = state.shape
    return pl.pallas_call(
        pack_kernel,
        out_shape=pltpu.VMEM((owners, count, variables, height * depth // owners, width), jnp.float32),
        in_specs=[pl.BlockSpec(memory_space=pl.ANY)] * 2,
        out_specs=pl.BlockSpec(memory_space=pltpu.VMEM),
        scratch_shapes=[pltpu.SemaphoreType.DMA((count, owners))],
        compiler_params=pltpu.CompilerParams(vmem_limit_bytes=61 * 2**20),
        cost_estimate=pl.CostEstimate(flops=0, bytes_accessed=8 * state.size, transcendentals=0),
    )(state, local)


def time_kernel(gathered_hbm, out_hbm, gathered_ref, done_ref, in_sems, out_sems):
    row = frequency * kernel_row(NT)
    lines = gathered_ref.shape[1] // WRITES
    rows = [slice(b * lines, (b + 1) * lines) for b in range(WRITES)]
    fetches = [
        pltpu.make_async_copy(gathered_hbm.at[:, r], gathered_ref.at[:, r], in_sems.at[b])
        for b, r in enumerate(rows)
    ]
    writes = [
        pltpu.make_async_copy(done_ref.at[:, r], out_hbm.at[:, r], out_sems.at[b]) for b, r in enumerate(rows)
    ]
    for fetch in fetches:
        fetch.start()
    for b in range(WRITES):
        fetches[b].wait()

        def step(tile, carry):
            at = pl.ds(pl.multiple_of(b * lines + tile * TILE, TILE), TILE)
            values = [gathered_ref[n, at, :] for n in range(NT)]
            for n, value in enumerate(circular_sums(values, row)):
                done_ref[n, at, :] = value
            return carry

        lax.fori_loop(0, lines // TILE, step, 0)
        writes[b].start()
    for write in writes:
        write.wait()


def time_terms(gathered):
    anywhere = pl.BlockSpec(memory_space=pl.ANY)
    return pl.pallas_call(
        time_kernel,
        out_shape=jax.ShapeDtypeStruct(gathered.shape, jnp.float32),
        in_specs=[anywhere],
        out_specs=anywhere,
        scratch_shapes=[
            pltpu.VMEM(gathered.shape, jnp.float32),
            pltpu.VMEM(gathered.shape, jnp.float32),
            pltpu.SemaphoreType.DMA((WRITES,)),
            pltpu.SemaphoreType.DMA((WRITES,)),
        ],
        compiler_params=pltpu.CompilerParams(vmem_limit_bytes=62 * 2**20),
        cost_estimate=pl.CostEstimate(
            flops=16 * gathered.size, bytes_accessed=8 * gathered.size, transcendentals=0
        ),
    )(gathered)


def primitives(q):
    inverse = 1.0 / q[0]
    speed = [q[1] * inverse, q[2] * inverse, q[3] * inverse]
    pressure = 0.4 * (q[4] - 0.5 * (q[1] * speed[0] + q[2] * speed[1] + q[3] * speed[2]))
    sound = jnp.sqrt(1.4 * pressure * inverse)
    return speed, pressure, sound


def along(speed, sound, normal):
    normal_speed = speed[0] * normal[0] + speed[1] * normal[1] + speed[2] * normal[2]
    area = jnp.sqrt(normal[0] * normal[0] + normal[1] * normal[1] + normal[2] * normal[2])
    return normal_speed, jnp.abs(normal_speed) + sound * area


def flux(v, q, normal_speed, pressure, normal):
    if v in (1, 2, 3):
        return q * normal_speed + pressure * normal[v - 1]
    if v == 4:
        return (q + pressure) * normal_speed
    return q * normal_speed


def cross_instance(n, writes, state_ref, metric_ref, volume_ref, out_ref, span_ref, out_hbm, sem):
    depth, height, width = state_ref.shape[2:]
    lane = lax.broadcasted_iota(jnp.int32, (height, width), 1)
    first = lane == 0
    last = lane == width - 1
    back = lambda x: pltpu.roll(x, 1, 1)
    ahead = lambda x: pltpu.roll(x, width - 1, 1)

    def prepare(k, carry):
        q = [state_ref[n, v, k] for v in range(6)]
        speed, pressure, sound = primitives(q)
        for v in range(3):
            span_ref[7 + v, k] = speed[v]
        span_ref[10, k] = pressure
        span_ref[11, k] = sound
        normal = [metric_ref[2, c, k] for c in range(3)]
        normal_speed, radius = along(speed, sound, normal)
        span_ref[6, k] = radius
        for v in range(6):
            span_ref[v, k] = flux(v, q[v], normal_speed, pressure, normal)
        return carry

    lax.fori_loop(0, depth, prepare, 0)

    def step(k, carry):
        speed = [span_ref[7 + v, k] for v in range(3)]
        pressure = span_ref[10, k]
        sound = span_ref[11, k]
        wall_normal = [metric_ref[1, c, k] for c in range(3)]
        wall_speed, wall_radius = along(speed, sound, wall_normal)
        wall_weight = dissipation * (wall_radius + jnp.where(first, wall_radius, back(wall_radius)))
        wall_end = (2.0 * dissipation) * wall_radius
        squared = (
            wall_normal[0] * wall_normal[0] + wall_normal[1] * wall_normal[1] + wall_normal[2] * wall_normal[2]
        )
        coefficient = viscosity * (1.0 + state_ref[n, 5, k]) * (squared / volume_ref[k])
        coefficient = coefficient + back(coefficient)
        k1 = jnp.maximum(k - 1, 0)
        k2 = jnp.maximum(k - 2, 0)
        k3 = jnp.minimum(k + 1, depth - 1)
        k4 = jnp.minimum(k + 2, depth - 1)
        span_low = dissipation * (span_ref[6, k] + span_ref[6, k1])
        span_high = dissipation * (span_ref[6, k] + span_ref[6, k3])
        for v in range(6):
            q = state_ref[n, v, k]
            cell = flux(v, q, wall_speed, pressure, wall_normal)
            step_one = jnp.where(first, 0.0, q - back(q))
            step_two = ahead(step_one) - step_one
            step_three = step_two - jnp.where(first, 0.0, back(step_two))
            face = cell + jnp.where(first, cell, back(cell)) - wall_weight * step_three
            if v > 0:
                face = face - coefficient * step_one
            end = 2.0 * cell - wall_end * step_one
            total = jnp.where(last, end, ahead(face)) - face
            q1 = state_ref[n, v, k1]
            q2 = state_ref[n, v, k2]
            q3 = state_ref[n, v, k3]
            q4 = state_ref[n, v, k4]
            total = total + (span_ref[v, k3] - span_ref[v, k1])
            total = total - span_high * (q4 - q1 - 3.0 * (q3 - q))
            total = total + span_low * (q3 - q2 - 3.0 * (q - q1))
            out_ref[v, k] = total
        return carry

    run = depth // writes

    def write(r, carry):
        lax.fori_loop(r * run, (r + 1) * run, step, 0)
        done = pltpu.make_async_copy(
            out_ref.at[:, pl.ds(r * run, run)], out_hbm.at[n, :, pl.ds(r * run, run)], sem
        )
        done.start()
        done.wait()
        return carry

    lax.fori_loop(0, writes, write, 0)


def cross_kernel(
    turn, writes, state_hbm, metric_hbm, volume_hbm, out_hbm,
    state_ref, metric_ref, volume_ref, out_ref, span_ref, in_sems, out_sem,
):
    count = state_ref.shape[0]

    @pl.when(lax.axis_index("wrap") % 2 == turn)
    def _():
        fetches = [
            pltpu.make_async_copy(metric_hbm, metric_ref, in_sems.at[0]),
            pltpu.make_async_copy(volume_hbm, volume_ref, in_sems.at[1]),
            pltpu.make_async_copy(state_hbm, state_ref, in_sems.at[2]),
        ]
        for fetch in fetches:
            fetch.start()
        for fetch in fetches:
            fetch.wait()

        for n in range(count):
            cross_instance(
                n, writes[n % len(writes)], state_ref, metric_ref, volume_ref, out_ref, span_ref, out_hbm, out_sem
            )


def cross(turn, writes, limit, state, metrics, volume):
    count, variables, depth, height, width = state.shape
    anywhere = pl.BlockSpec(memory_space=pl.ANY)
    slabs = lambda size: pltpu.VMEM((size, depth, height, width), jnp.float32)
    return pl.pallas_call(
        functools.partial(cross_kernel, turn, writes),
        out_shape=jax.ShapeDtypeStruct(state.shape, jnp.float32),
        in_specs=[anywhere] * 3,
        out_specs=anywhere,
        scratch_shapes=[
            pltpu.VMEM(state.shape, jnp.float32),
            pltpu.VMEM(metrics.shape, jnp.float32),
            pltpu.VMEM(volume.shape, jnp.float32),
            slabs(variables),
            slabs(12),
            pltpu.SemaphoreType.DMA((3,)),
            pltpu.SemaphoreType.DMA(()),
        ],
        compiler_params=pltpu.CompilerParams(vmem_limit_bytes=limit * 2**20),
        cost_estimate=pl.CostEstimate(
            flops=300 * count * depth * height * width,
            bytes_accessed=12 * state.size + 4 * metrics.size,
            transcendentals=0,
        ),
    )(state, metrics, volume)


def wrap_kernel(
    state_ref, halo_ref, metric_ref, metric_halo_ref, early_hbm, late_hbm, out_ref, cross_ref, sem
):
    depth, height, width = state_ref.shape[2:]
    n = pl.program_id(0)
    rows = height + TILE
    down = lambda x: pltpu.roll(x, 1, 0)
    up = lambda x: pltpu.roll(x, rows - 1, 0)
    join = lambda a, b: jnp.concatenate([a, b], axis=0)
    for turn, ref in enumerate([early_hbm, late_hbm]):

        @pl.when(lax.axis_index("wrap") % 2 == turn)
        def _():
            fetch = pltpu.make_async_copy(ref.at[n], cross_ref, sem)
            fetch.start()
            fetch.wait()

    def step(k, carry):
        q = [join(state_ref[n, v, k], halo_ref[n, v, k]) for v in range(6)]
        speed, pressure, sound = primitives(q)
        normal = [join(metric_ref[0, c, k], metric_halo_ref[c, k]) for c in range(3)]
        normal_speed, radius = along(speed, sound, normal)
        weight = dissipation * (radius + down(radius))
        for v in range(6):
            face = flux(v, q[v], normal_speed, pressure, normal)
            step_one = q[v] - down(q[v])
            step_two = up(step_one) - step_one
            step_three = step_two - down(step_two)
            face = face + down(face) - weight * step_three
            out_ref[n, v, k] = cross_ref[v, k] + (up(face) - face)[:height]
        return carry

    lax.fori_loop(0, depth, step, 0)


def with_wrap(state, halo, metrics, metric_halo, early, late):
    vmem = pl.BlockSpec(memory_space=pltpu.VMEM)
    return pl.pallas_call(
        wrap_kernel,
        grid=(state.shape[0],),
        out_shape=jax.ShapeDtypeStruct(state.shape, jnp.float32),
        in_specs=[vmem] * 4 + [pl.BlockSpec(memory_space=pl.ANY)] * 2,
        out_specs=vmem,
        scratch_shapes=[pltpu.VMEM(state.shape[1:], jnp.float32), pltpu.SemaphoreType.DMA(())],
        compiler_params=pltpu.CompilerParams(vmem_limit_bytes=16 * 2**20),
        cost_estimate=pl.CostEstimate(
            flops=30 * state.size, bytes_accessed=12 * state.size + 4 * metrics.size, transcendentals=0
        ),
    )(state, halo, metrics, metric_halo, early, late)


def combine_kernel(spatial_ref, volume_ref, term_hbm, out_hbm, term_ref, done_ref, in_sems, out_sems):
    count, variables, depth = spatial_ref.shape[:3]
    parts = term_ref.shape[0] // depth
    run = variables // BLOCKS
    blocks = [(n, slice(b * run, (b + 1) * run)) for n in range(count) for b in range(BLOCKS)]
    fetches = [
        pltpu.make_async_copy(term_hbm.at[:, n, r], term_ref.at[:, n, r], in_sems.at[b])
        for b, (n, r) in enumerate(blocks)
    ]
    writes = [
        pltpu.make_async_copy(done_ref.at[n, r], out_hbm.at[n, r], out_sems.at[b])
        for b, (n, r) in enumerate(blocks)
    ]
    for fetch in fetches:
        fetch.start()
    for b, (n, r) in enumerate(blocks):
        fetches[b].wait()

        def step(k, carry):
            volume = volume_ref[k]
            for v in range(r.start, r.stop):
                term = jnp.concatenate([term_ref[parts * k + p, n, v] for p in range(parts)], axis=0)
                done_ref[n, v, k] = spatial_ref[n, v, k] + volume * term
            return carry

        lax.fori_loop(0, depth, step, 0)
        writes[b].start()
    for write in writes:
        write.wait()


def combined(local, volume, terms):
    vmem = pl.BlockSpec(memory_space=pltpu.VMEM)
    anywhere = pl.BlockSpec(memory_space=pl.ANY)
    count = local.shape[0] * BLOCKS
    return pl.pallas_call(
        combine_kernel,
        out_shape=jax.ShapeDtypeStruct(local.shape, jnp.float32),
        in_specs=[vmem] * 2 + [anywhere],
        out_specs=anywhere,
        scratch_shapes=[
            pltpu.VMEM(terms.shape, jnp.float32),
            pltpu.VMEM(local.shape, jnp.float32),
            pltpu.SemaphoreType.DMA((count,)),
            pltpu.SemaphoreType.DMA((count,)),
        ],
        compiler_params=pltpu.CompilerParams(vmem_limit_bytes=16 * 2**20),
        cost_estimate=pl.CostEstimate(
            flops=2 * local.size, bytes_accessed=12 * local.size, transcendentals=0
        ),
    )(local, volume, terms)


def wrap_halos(state, metrics):
    count = lax.axis_size("wrap")
    onward = [(i, (i + 1) % count) for i in range(count)]
    backward = [((i + 1) % count, i) for i in range(count)]
    inst_count, variables, depth, height, width = state.shape
    pack = lambda cells, face: jnp.concatenate(
        [cells.reshape(-1, width), face.reshape(-1, width)], axis=0
    )
    size = inst_count * variables * depth * 2
    before = lax.ppermute(pack(state[..., -2:, :], metrics[0, :, :, -1:]), "wrap", onward)
    after = lax.ppermute(pack(state[..., :2, :], metrics[0, :, :, :1]), "wrap", backward)
    cells = lambda packed: packed[:size].reshape(inst_count, variables, depth, 2, width)
    face = lambda packed: packed[size:].reshape(3, depth, 1, width)
    halo = jnp.concatenate([cells(after), cells(after), cells(before), cells(before)], axis=-2)
    metric_halo = jnp.concatenate([face(after)] * 4 + [face(before)] * 4, axis=-2)
    return halo, metric_halo


def body(state, metrics, volume):
    inst_count, variables, depth, height, width = state.shape
    owners = lax.axis_size("inst")
    parts = owners // depth
    lines = height // parts
    early = cross(0, EARLY, FIRST, state, metrics, volume)
    sent = packed(state, early, owners).reshape(owners, inst_count * variables * lines, width)
    held = lax.all_to_all(sent, "inst", 0, 0, tiled=True)
    terms = time_terms(held.reshape(owners * inst_count, variables * lines, width))
    terms = lax.all_to_all(terms.reshape(sent.shape), "inst", 0, 0, tiled=True)
    terms = terms.reshape(owners, inst_count, variables, lines, width)
    late = cross(1, LATE, SECOND, state, metrics, volume)
    after, late = lax.optimization_barrier((state, late))
    halo, metric_halo = wrap_halos(after, metrics)
    local = with_wrap(state, halo, metrics, metric_halo, early, late)
    return combined(0.5 * local, volume, terms)


def solution(mesh):
    in_specs = (
        P("inst", None, None, "wrap", None),
        P(None, None, None, "wrap", None),
        P(None, "wrap", None),
    )
    out_specs = P("inst", None, None, "wrap", None)
    return jax.shard_map(body, mesh=mesh, in_specs=in_specs, out_specs=out_specs, check_vma=False)
```
